512 devices in a mesh: pipe: 32 (over z, x_lo), dp: 16 (over y, x_hi, core).
Axes of the slice: x: 4 (x_hi: 2, x_lo: 2; x = x_hi * 2 + x_lo), y: 4, z: 16, core: 2. Of those that a mesh axis runs over, the one named last changes fastest.
Arguments:
- fwd_in: bfloat16 [32, 2, 256, 7168], P('pipe', None, None, 'dp'), may hold values from -6 to 6
- stash: bfloat16 [32, 2, 256, 7168], P('pipe', None, None, 'dp'), may hold values from -6 to 6
- cot_in: bfloat16 [32, 2, 256, 7168], P('pipe', None, None, 'dp'), may hold values from -6 to 6
- w_down: bfloat16 [32, 2, 7168, 512], P('pipe', None, 'dp'), may hold values from -0.04783613 to 0.04783613, as said below
- w_up: bfloat16 [32, 2, 512, 7168], P('pipe', None, None, 'dp'), may hold values from -0.1789864 to 0.1789864, as said below
- gain: float32 [32, 2, 7168], P('pipe', None, 'dp'), may hold values from 0.5 to 2, as said below
Outputs:
- fwd_next: bfloat16 [32, 2, 256, 7168], P('pipe', None, None, 'dp')
- bwd_next: bfloat16 [32, 2, 256, 7168], P('pipe', None, None, 'dp')
- grad_down: bfloat16 [32, 7168, 512], P('pipe', 'dp')
- grad_up: bfloat16 [32, 512, 7168], P('pipe', None, 'dp')
- grad_gain: bfloat16 [32, 7168], P('pipe', 'dp')
The draws below stay inside these ranges and needn't reach their ends.
Inputs may be any that keep to these rules, and one draw needn't show every extreme that they name: w_down[s, 1] equals w_down[31 - s, 0] for every position s: both slots hold copies of sections. w_up[s, 1] equals w_up[31 - s, 0] for every position s. gain[s, 1] equals gain[31 - s, 0] for every position s.
All inputs are finite; a program needn't handle non-finite values.
Results may differ from the reference program's by a relative error of at most 0.02.
Values may be sent and summed in bfloat16 or wider, within the bound.
A program may use at most 64 MiB of HBM per device.

```python
import jax
import jax.numpy as jnp
from jax import lax

D = 7168
R = 512
TOKENS = 256
N_PIPE = 32


def mirrored(values):
    return jnp.stack([values, values[::-1]], axis=1)


def draw_w_down(key, part):
    key = jax.random.fold_in(key, 11)
    section_weights = jax.random.truncated_normal(key, -4.0, 4.0, (N_PIPE, D, R), jnp.float32)
    return mirrored(section_weights * D ** (-0.5)).astype(jnp.bfloat16)


def draw_w_up(key, part):
    key = jax.random.fold_in(key, 23)
    section_weights = jax.random.truncated_normal(key, -4.0, 4.0, (N_PIPE, R, D), jnp.float32)
    return mirrored(section_weights * R ** (-0.5)).astype(jnp.bfloat16)


def draw_gain(key, part):
    key = jax.random.fold_in(key, 37)
    section_gains = jnp.exp(jax.random.uniform(key, (N_PIPE, D), jnp.float32, -0.69, 0.69))
    return mirrored(section_gains)


def levels(rng, dims, cuts, smallest, top_value):
    factor_of = 1.0
    for axis_at, blocks in cuts:
        steps = jax.random.uniform(jax.random.fold_in(jax.random.fold_in(rng, 6), axis_at), (blocks,), jnp.float32, smallest / len(cuts), top_value / len(cuts))
        factor_of = factor_of * jnp.repeat(jnp.exp(steps), dims[axis_at] // blocks).reshape((-1,) + (1,) * (len(dims) - 1 - axis_at))
    return factor_of


def normal_values(stream_key, dims, scale, limit, pieces=(), held_as=jnp.bfloat16):
    drawn = scale * jax.random.normal(stream_key, dims, jnp.float32)
    if pieces:
        drawn = drawn * levels(stream_key, dims, pieces, -0.22, 0.18)
    return jnp.clip(drawn, -limit, limit).astype(held_as)


def setup_inputs(seed: int = 0) -> dict:
    keys = jax.random.split(jax.random.key(seed), 7)
    fwd_in = normal_values(keys[0], (N_PIPE, 2, TOKENS, D), 1.0, 6.0, ((0, 32), (3, 16)))
    stash = normal_values(keys[1], (N_PIPE, 2, TOKENS, D), 1.0, 6.0, ((0, 32), (3, 16)))
    cot_in = normal_values(keys[2], (N_PIPE, 2, TOKENS, D), 1.0, 6.0, ((0, 32), (3, 16)))
    w_down = draw_w_down(jax.random.fold_in(keys[6], 71), 0)
    w_up = draw_w_up(jax.random.fold_in(keys[6], 71), 0)
    gain = draw_gain(jax.random.fold_in(keys[6], 71), 0)
    return {"fwd_in": fwd_in, "stash": stash, "cot_in": cot_in, "w_down": w_down, "w_up": w_up, "gain": gain}


EPS = 1e-06

def forward_parts(rows, w_down, gain):
    wide = rows.astype(jnp.float32)
    inv_rms = lax.rsqrt(lax.optimization_barrier(jnp.mean(wide * wide, axis=-1, keepdims=True)) + EPS)
    normed = (wide * inv_rms).astype(jnp.bfloat16)
    scaled = (normed.astype(jnp.float32) * gain).astype(jnp.bfloat16)
    latent = jnp.dot(scaled, w_down, preferred_element_type=jnp.float32)
    lat_inv = lax.rsqrt(lax.optimization_barrier(jnp.mean(latent * latent, axis=-1, keepdims=True)) + EPS)
    lat_unit = latent * lat_inv
    lat_rows = lat_unit.astype(jnp.bfloat16)
    return (wide, inv_rms, normed, scaled, lat_inv, lat_unit, lat_rows)

def section_forward(rows, w_down, w_up, gain):
    wide, inv_rms, normed, scaled, lat_inv, lat_unit, lat_rows = forward_parts(rows, w_down, gain)
    branch = jnp.dot(lat_rows, w_up, preferred_element_type=jnp.float32).astype(jnp.bfloat16)
    return (wide + branch.astype(jnp.float32)).astype(jnp.bfloat16)

def section_backward(rows, cotangent, w_down, w_up, gain, factor):
    wide, inv_rms, normed, scaled, lat_inv, lat_unit, lat_rows = forward_parts(rows, w_down, gain)
    up_grad = jnp.dot(lat_rows.T, cotangent, preferred_element_type=jnp.float32)
    lat_cot = jnp.dot(cotangent, w_up.T, preferred_element_type=jnp.float32)
    latent_cot = lat_inv * (lat_cot - lat_unit * lax.optimization_barrier(jnp.mean(lat_cot * lat_unit, axis=-1, keepdims=True)))
    latent_cot = latent_cot.astype(jnp.bfloat16)
    down_grad = jnp.dot(scaled.T, latent_cot, preferred_element_type=jnp.float32)
    scaled_cot = jnp.dot(latent_cot, w_down.T, preferred_element_type=jnp.float32)
    gain_grad = lax.optimization_barrier(jnp.sum(normed.astype(jnp.float32) * scaled_cot, axis=0))
    normed_cot = (scaled_cot * gain).astype(jnp.bfloat16).astype(jnp.float32)
    unit_rows = wide * inv_rms
    input_cot = cotangent.astype(jnp.float32) + inv_rms * (normed_cot - unit_rows * lax.optimization_barrier(jnp.mean(normed_cot * unit_rows, axis=-1, keepdims=True)))
    return (input_cot.astype(jnp.bfloat16), (down_grad * factor).astype(jnp.bfloat16), (up_grad * factor).astype(jnp.bfloat16), (gain_grad * factor).astype(jnp.bfloat16))

def reference(fwd_in, stash, cot_in, w_down, w_up, gain):
    factor = TOKENS ** (-0.5)

    def per_position(items):
        inputs, stored, cotangent, downs, ups, gains = items
        outputs = []
        backs = []
        for slot in range(2):
            outputs.append(section_forward(inputs[slot], downs[slot], ups[slot], gains[slot]))
            backs.append(section_backward(stored[slot], cotangent[slot], downs[slot], ups[slot], gains[slot], factor))
        return (jnp.stack(outputs), jnp.stack([entry[0] for entry in backs]), jnp.stack([entry[1] for entry in backs]), jnp.stack([entry[2] for entry in backs]), jnp.stack([entry[3] for entry in backs]))
    outputs, input_cots, copy_down, copy_up, copy_gain = lax.map(per_position, (fwd_in, stash, cot_in, w_down, w_up, gain))
    zero_rows = jnp.zeros((1,) + outputs.shape[2:], jnp.bfloat16)
    fwd_next = jnp.stack([jnp.concatenate([zero_rows, outputs[:-1, 0]], axis=0), jnp.concatenate([outputs[1:, 1], zero_rows], axis=0)], axis=1)
    bwd_next = jnp.stack([jnp.concatenate([input_cots[1:, 0], zero_rows], axis=0), jnp.concatenate([zero_rows, input_cots[:-1, 1]], axis=0)], axis=1)
    grad_down = (copy_down[:, 0].astype(jnp.float32) + copy_down[::-1, 1].astype(jnp.float32)).astype(jnp.bfloat16)
    grad_up = (copy_up[:, 0].astype(jnp.float32) + copy_up[::-1, 1].astype(jnp.float32)).astype(jnp.bfloat16)
    grad_gain = (copy_gain[:, 0].astype(jnp.float32) + copy_gain[::-1, 1].astype(jnp.float32)).astype(jnp.bfloat16)
    return (fwd_next, bwd_next, grad_down, grad_up, grad_gain)
```

```python
import functools

import jax
import jax.numpy as jnp
from jax import lax
from jax.experimental import pallas as pl
from jax.experimental.pallas import tpu as pltpu
from jax.sharding import PartitionSpec as P

MESH = pl.DeviceIdType.MESH
EPS = 1e-06
BF16 = jnp.bfloat16
F32 = jnp.float32

Y, XH, CORE = 4, 2, 2


def dot(a, b, ca, cb):
    return lax.dot_general(a, b, (((ca,), (cb,)), ((), ())), preferred_element_type=F32)


def kernel(
    n_pipe,
    fwd_ref,
    stash_ref,
    cot_ref,
    wd_ref,
    wu_ref,
    gain_ref,
    fwd_out,
    bwd_out,
    gd_out,
    gu_out,
    gg_out,
    part,
    r1,
    r2,
    h2,
    r3,
    full,
    zg,
    tail,
    mz,
    md,
    mt,
    gsend,
    grecv,
    rows_out,
    down_acc,
    up_acc,
    core_s,
    core_r,
    y_s,
    y_r,
    x_s,
    x_r,
    gx_s,
    gx_r,
    gy_s,
    gy_r,
    gc_s,
    gc_r,
    m_s,
    m_r,
    n_s,
    n_r,
    zero_sem,
):
    pos = lax.axis_index("pipe")
    d = lax.axis_index("dp")
    tokens, cols = stash_ref.shape[1:]
    lat = wd_ref.shape[2]
    features = cols * Y * XH * CORE
    two = 2 * lat
    main = cols // 128 * 128
    rest = cols - main
    half, quarter, own = tokens // 2, tokens // 8, tokens // 16
    core = d % CORE
    xh = d // CORE % XH
    y = d // (CORE * XH)
    sibling = (pos, d + 1 - 2 * core)
    across = (pos, d + CORE * (1 - 2 * xh))
    ring = [(pos, (y + k) % Y * (CORE * XH) + d % (CORE * XH)) for k in range(1, Y)]
    mirror = (n_pipe - 1 - pos, d)
    above = ((pos + 1) % n_pipe, d)
    below = ((pos + n_pipe - 1) % n_pipe, d)

    def send(src, dst, s_sem, r_sem, device):
        return pltpu.make_async_remote_copy(
            src_ref=src,
            dst_ref=dst,
            send_sem=s_sem,
            recv_sem=r_sem,
            device_id=device,
            device_id_type=MESH,
        )

    barrier = pltpu.get_barrier_semaphore()
    partners = [sibling, across, *ring, mirror, above, below]
    for device in partners:
        pl.semaphore_signal(barrier, inc=1, device_id=device, device_id_type=MESH)
    pl.semaphore_wait(barrier, len(partners))

    mirror_dy = send(cot_ref.at[1, :, :main], md, m_s.at[0], m_r.at[0], mirror)
    mirror_dy.start()
    wide1 = stash_ref[1].astype(F32)
    scaled1 = wide1 * gain_ref[1:2, :]
    zg[1] = scaled1.astype(BF16)
    mirror_z = send(zg.at[1, :, :main], mz, m_s.at[1], m_r.at[1], mirror)
    mirror_z.start()
    tail[...] = jnp.concatenate(
        [cot_ref[1, :, main:].astype(F32), scaled1[:, main:]], axis=1
    ).astype(BF16)
    mirror_t = send(tail, mt, m_s.at[2], m_r.at[2], mirror)
    mirror_t.start()

    def squares(wide):
        return jnp.sum(wide * wide, axis=1, keepdims=True)

    core_copies = []

    def core_send(g):
        away = pl.multiple_of((1 - core) * half, half)
        copy = send(part.at[g, pl.ds(away, half), :], r1.at[g], core_s.at[g], core_r.at[g], sibling)
        copy.start()
        core_copies.append(copy)

    for g, slot in ((0, 1), (1, 0)):
        wide = stash_ref[slot].astype(F32)
        if slot == 0:
            zg[0] = (wide * gain_ref[0:1, :]).astype(BF16)
        part[g, :, :lat] = dot(zg[slot], wd_ref[slot], 1, 0).astype(BF16)
        part[g, :, lat:two] = dot(cot_ref[slot], wu_ref[slot], 1, 1).astype(BF16)
        part[g, :, two:] = jnp.broadcast_to(squares(wide), (tokens, 128)).astype(BF16)
        core_send(g)
    norms = []
    for slot in range(2):
        wide = fwd_ref[slot].astype(F32)
        norms.append(squares(wide))
        rows = (wide * gain_ref[slot : slot + 1, :]).astype(BF16)
        part[2, :, slot * lat : (slot + 1) * lat] = dot(rows, wd_ref[slot], 1, 0).astype(BF16)
    lane = lax.broadcasted_iota(jnp.int32, (tokens, 128), 1)
    part[2, :, two:] = jnp.where(lane < 64, norms[0], norms[1]).astype(BF16)
    core_send(2)

    ring_copies = []
    for g in range(3):
        core_copies[g].wait_recv()
        mine = part[g, pl.ds(pl.multiple_of(core * half, half), half), :].astype(F32)
        r1[g] = (mine + r1[g].astype(F32)).astype(BF16)
        for k in range(1, Y):
            to = pl.multiple_of((y + k) % Y * quarter, quarter)
            copy = send(
                r1.at[g, pl.ds(to, quarter), :],
                r2.at[g, k - 1],
                y_s.at[g, k - 1],
                y_r.at[g, k - 1],
                ring[k - 1],
            )
            copy.start()
            ring_copies.append(copy)
    x_copies = []
    for g in range(3):
        total = r1[g, pl.ds(pl.multiple_of(y * quarter, quarter), quarter), :].astype(F32)
        for k in range(Y - 1):
            ring_copies[g * 3 + k].wait_recv()
            total = total + r2[g, k].astype(F32)
        h2[g] = total.astype(BF16)
        copy = send(
            h2.at[g, pl.ds(pl.multiple_of((1 - xh) * own, own), own), :],
            r3.at[g],
            x_s.at[g],
            x_r.at[g],
            across,
        )
        copy.start()
        x_copies.append(copy)

    base = pl.multiple_of(core * half + y * quarter + xh * own, own)
    block = pl.multiple_of(core * half + y * quarter, quarter)

    def mean_sq(values):
        return jnp.sum(values * values, axis=1, keepdims=True) / lat

    mirror_rows = send(
        full.at[0, pl.ds(base, own), :two],
        full.at[3, pl.ds(base, own), :two],
        m_s.at[3],
        m_r.at[3],
        mirror,
    )
    gx_copies = {}
    widths = (two + 128, two + 128, two, two)

    def gx_send(g):
        spot = full.at[g, pl.ds(base, own), : widths[g]]
        gx_copies[g] = send(spot, spot, gx_s.at[g], gx_r.at[g], across)
        gx_copies[g].start()

    for g in range(3):
        x_copies[g].wait_recv()
        total = h2[g, pl.ds(pl.multiple_of(xh * own, own), own), :].astype(F32) + r3[g].astype(F32)
        first, second = total[:, :lat], total[:, lat:two]
        square = total[:, two : two + 1] / features + EPS
        scale = lax.rsqrt(mean_sq(first) + EPS * square)
        unit = first * scale
        full[g, pl.ds(base, own), :lat] = unit.astype(BF16)
        if g < 2:
            mean = jnp.sum(second * unit, axis=1, keepdims=True) / lat
            cot = (scale * (second - unit * mean)).astype(BF16)
            full[g, pl.ds(base, own), lat:two] = cot
            pull = jnp.sum(cot.astype(F32) * first, axis=1, keepdims=True) / (features * square)
            full[g, pl.ds(base, own), two:] = jnp.broadcast_to(pull, (own, 128)).astype(BF16)
        else:
            square = total[:, two + 64 : two + 65] / features + EPS
            scale = lax.rsqrt(mean_sq(second) + EPS * square)
            full[g, pl.ds(base, own), lat:two] = (second * scale).astype(BF16)
        if g == 0:
            mirror_rows.start()
        gx_send(g)

    gy_copies, gc_copies = {}, {}

    def gc_send(g, index, row):
        spot = full.at[g, pl.ds(row, quarter), : widths[g]]
        gc_copies[g, index] = send(spot, spot, gc_s.at[g, index], gc_r.at[g, index], sibling)
        gc_copies[g, index].start()

    def gy_send(g):
        gx_copies[g].wait_recv()
        spot = full.at[g, pl.ds(block, quarter), : widths[g]]
        for k in range(1, Y):
            gy_copies[g, k] = send(spot, spot, gy_s.at[g, k - 1], gy_r.at[g, k - 1], ring[k - 1])
            gy_copies[g, k].start()
        gc_send(g, 0, block)

    def gy_pass(g):
        for k in range(1, Y):
            gy_copies[g, k].wait_recv()
            row = pl.multiple_of(core * half + (y + Y - k) % Y * quarter, quarter)
            gc_send(g, k, row)

    def gc_wait(g):
        for k in range(Y):
            gc_copies[g, k].wait_recv()

    ups = (pos < n_pipe - 1, pos > 0)

    def relay(index, slot, out, up):
        return send(rows_out.at[index], out.at[slot], n_s.at[index], n_r.at[index], above if up else below)

    relays = [relay(0, 1, bwd_out, True), relay(1, 0, bwd_out, False), relay(2, 0, fwd_out, True), relay(3, 1, fwd_out, False)]

    def relay_start(index):
        @pl.when(ups[index % 2])
        def _():
            relays[index].start()

    for g in range(3):
        gy_send(g)
    for g in range(3):
        gy_pass(g)

    mirror_gain = send(gsend, grecv, m_s.at[4], m_r.at[4], mirror)
    gain_sum = None
    for g, slot in ((0, 1), (1, 0)):
        gc_wait(g)
        scaled_cot = dot(full[g, :, lat:two], wd_ref[slot], 1, 1)
        wide = stash_ref[slot].astype(F32)
        pull = full[g, :, two : two + 1].astype(F32)
        rows_out[g] = (
            cot_ref[slot].astype(F32) + scaled_cot * gain_ref[slot : slot + 1, :] - wide * pull
        ).astype(BF16)
        relay_start(g)
        gain_rows = jnp.sum(wide * scaled_cot, axis=0, keepdims=True)
        if slot == 1:
            gsend[...] = jnp.broadcast_to(gain_rows, gsend.shape)
            mirror_gain.start()
        else:
            gain_sum = gain_rows
    gc_wait(2)
    for slot in range(2):
        branch = dot(full[2, :, slot * lat : (slot + 1) * lat], wu_ref[slot], 1, 0).astype(BF16)
        rows_out[2 + slot] = (fwd_ref[slot].astype(F32) + branch.astype(F32)).astype(BF16)
        relay_start(2 + slot)

    mirror_rows.wait_recv()
    gx_send(3)
    down_acc[...] = dot(zg[0], full[1, :, lat:two], 0, 0)
    gy_send(3)
    up_acc[...] = dot(full[1, :, :lat], cot_ref[0], 0, 0)
    gy_pass(3)
    gc_wait(3)

    factor = tokens ** (-0.5)
    mirror_dy.wait_recv()
    up = up_acc[:, :main] + dot(full[3, :, :lat], md[...], 0, 0)
    gu_out[:, :main] = (up * factor).astype(BF16)
    mirror_z.wait_recv()
    down = down_acc[:main, :] + dot(mz[...], full[3, :, lat:two], 0, 0)
    gd_out[:main, :] = (down * factor).astype(BF16)
    mirror_t.wait_recv()
    up = up_acc[:, main:] + dot(full[3, :, :lat], mt[...], 0, 0)[:, :rest]
    gu_out[:, main:] = (up * factor).astype(BF16)
    down = down_acc[main:, :] + dot(mt[...], full[3, :, lat:two], 0, 0)[rest:, :]
    gd_out[main:, :] = (down * factor).astype(BF16)
    mirror_gain.wait_recv()
    gg_out[...] = ((gain_sum + grecv[0:1, :]) * factor).astype(BF16)

    def edge(here, first, second):
        @pl.when(here)
        def _():
            zg[0] = jnp.zeros((tokens, cols), BF16)
            one = pltpu.make_async_copy(zg.at[0], first, zero_sem.at[0])
            other = pltpu.make_async_copy(zg.at[0], second, zero_sem.at[1])
            one.start()
            other.start()
            one.wait()
            other.wait()

    edge(pos == 0, fwd_out.at[0], bwd_out.at[1])
    edge(pos == n_pipe - 1, fwd_out.at[1], bwd_out.at[0])

    for index in range(4):
        @pl.when(ups[index % 2])
        def _():
            relays[index].wait_send()

        @pl.when(ups[1 - index % 2])
        def _():
            relays[index].wait_recv()

    for copy in [
        mirror_dy,
        mirror_z,
        mirror_t,
        mirror_rows,
        mirror_gain,
        *core_copies,
        *ring_copies,
        *x_copies,
        *gx_copies.values(),
        *gy_copies.values(),
        *gc_copies.values(),
    ]:
        copy.wait_send()


def per_device(n_pipe, fwd_in, stash, cot_in, w_down, w_up, gain):
    tokens, cols = stash.shape[2:]
    lat = w_down.shape[3]
    wide = 2 * lat + 128
    main = cols // 128 * 128
    half, quarter, own = tokens // 2, tokens // 8, tokens // 16
    vmem = pl.BlockSpec(memory_space=pltpu.VMEM)
    anywhere = pl.BlockSpec(memory_space=pl.ANY)
    dma = pltpu.SemaphoreType.DMA
    outs = pl.pallas_call(
        functools.partial(kernel, n_pipe),
        out_shape=(
            jax.ShapeDtypeStruct((2, tokens, cols), BF16),
            jax.ShapeDtypeStruct((2, tokens, cols), BF16),
            jax.ShapeDtypeStruct((cols, lat), BF16),
            jax.ShapeDtypeStruct((lat, cols), BF16),
            jax.ShapeDtypeStruct((1, cols), BF16),
        ),
        in_specs=[vmem] * 6,
        out_specs=(anywhere, anywhere, vmem, vmem, vmem),
        scratch_shapes=[
            pltpu.VMEM((3, tokens, wide), BF16),
            pltpu.VMEM((3, half, wide), BF16),
            pltpu.VMEM((3, Y - 1, quarter, wide), BF16),
            pltpu.VMEM((3, quarter, wide), BF16),
            pltpu.VMEM((3, own, wide), BF16),
            pltpu.VMEM((4, tokens, wide), BF16),
            pltpu.VMEM((2, tokens, cols), BF16),
            pltpu.VMEM((tokens, 128), BF16),
            pltpu.VMEM((tokens, main), BF16),
            pltpu.VMEM((tokens, main), BF16),
            pltpu.VMEM((tokens, 128), BF16),
            pltpu.VMEM((8, cols), F32),
            pltpu.VMEM((8, cols), F32),
            pltpu.VMEM((4, tokens, cols), BF16),
            pltpu.VMEM((cols, lat), F32),
            pltpu.VMEM((lat, cols), F32),
            dma((3,)),
            dma((3,)),
            dma((3, Y - 1)),
            dma((3, Y - 1)),
            dma((3,)),
            dma((3,)),
            dma((4,)),
            dma((4,)),
            dma((4, Y - 1)),
            dma((4, Y - 1)),
            dma((4, Y)),
            dma((4, Y)),
            dma((5,)),
            dma((5,)),
            dma((4,)),
            dma((4,)),
            dma((2,)),
        ],
        compiler_params=pltpu.CompilerParams(
            collective_id=0, has_side_effects=True, vmem_limit_bytes=40 * 1024 * 1024
        ),
    )(fwd_in[0], stash[0], cot_in[0], w_down[0], w_up[0], gain[0])
    fwd_next, bwd_next, grad_down, grad_up, grad_gain = outs
    return (fwd_next[None], bwd_next[None], grad_down[None], grad_up[None], grad_gain)


def solution(mesh):
    placed = (
        P("pipe", None, None, "dp"),
        P("pipe", None, None, "dp"),
        P("pipe", None, None, "dp"),
        P("pipe", None, "dp", None),
        P("pipe", None, None, "dp"),
        P("pipe", None, "dp"),
    )
    return jax.shard_map(
        functools.partial(per_device, mesh.shape["pipe"]),
        mesh=mesh,
        in_specs=placed,
        out_specs=(
            P("pipe", None, None, "dp"),
            P("pipe", None, None, "dp"),
            P("pipe", "dp", None),
            P("pipe", None, "dp"),
            P("pipe", "dp"),
        ),
        check_vma=False,
    )
```

```python
import functools

import jax
import jax.numpy as jnp
from jax import lax
from jax.experimental import pallas as pl
from jax.experimental.pallas import tpu as pltpu
from jax.sharding import PartitionSpec as P

MESH = pl.DeviceIdType.MESH
EPS = 1e-06
BF16 = jnp.bfloat16
F32 = jnp.float32

Y, XH, CORE = 4, 2, 2


def dot(a, b, ca, cb):
    return lax.dot_general(a, b, (((ca,), (cb,)), ((), ())), preferred_element_type=F32)


def kernel(
    n_pipe,
    fwd_hbm,
    stash_hbm,
    cot_hbm,
    wd_hbm,
    wu_hbm,
    gain_ref,
    fwd_out,
    bwd_out,
    gd_out,
    gu_out,
    gg_out,
    fwd_ref,
    stash_ref,
    cot_ref,
    wd_ref,
    wu_ref,
    part,
    r1,
    ra,
    rb,
    fa,
    fb,
    h2,
    r3,
    full,
    zg,
    mz,
    md,
    gsend,
    grecv,
    rows_out,
    down_acc,
    up_acc,
    in_sem,
    core_s,
    core_r,
    ya_s,
    ya_r,
    yb_s,
    yb_r,
    x_s,
    x_r,
    gx_s,
    gx_r,
    gy_s,
    gy_r,
    gc_s,
    gc_r,
    m_s,
    m_r,
    n_s,
    n_r,
    zero_sem,
):
    pos = lax.axis_index("pipe")
    d = lax.axis_index("dp")
    cols, tokens = stash_ref.shape[1:]
    lat = wd_ref.shape[2]
    features = cols * Y * XH * CORE
    two = 2 * lat
    half, quarter, own = tokens // 2, tokens // 8, tokens // 16
    core = d % CORE
    xh = d // CORE % XH
    y = d // (CORE * XH)
    sibling = (pos, d + 1 - 2 * core)
    across = (pos, d + CORE * (1 - 2 * xh))
    y1, y2, y3 = y + 1 - 2 * (y % 2), (y + 2) % Y, Y - 1 - y
    side1 = (pos, y1 * (CORE * XH) + d % (CORE * XH))
    side3 = (pos, y3 * (CORE * XH) + d % (CORE * XH))
    mirror = (n_pipe - 1 - pos, d)
    above = ((pos + 1) % n_pipe, d)
    below = ((pos + n_pipe - 1) % n_pipe, d)

    def send(src, dst, s_sem, r_sem, device):
        return pltpu.make_async_remote_copy(
            src_ref=src,
            dst_ref=dst,
            send_sem=s_sem,
            recv_sem=r_sem,
            device_id=device,
            device_id_type=MESH,
        )

    loads = {}
    for index, (name, src, dst) in enumerate(
        (
            ("cot1", cot_hbm.at[1], cot_ref.at[1]),
            ("stash1", stash_hbm.at[1], stash_ref.at[1]),
            ("wd", wd_hbm, wd_ref),
            ("wu", wu_hbm, wu_ref),
            ("stash0", stash_hbm.at[0], stash_ref.at[0]),
            ("cot0", cot_hbm.at[0], cot_ref.at[0]),
            ("fwd", fwd_hbm, fwd_ref),
        )
    ):
        loads[name] = pltpu.make_async_copy(src, dst, in_sem.at[index])
        loads[name].start()

    barrier = pltpu.get_barrier_semaphore()
    partners = [sibling, across, side1, side3, mirror, above, below]
    for device in partners:
        pl.semaphore_signal(barrier, inc=1, device_id=device, device_id_type=MESH)

    def column(slot):
        wide = jnp.broadcast_to(gain_ref[slot : slot + 1, :], (128, cols)).T
        return jnp.concatenate([wide] * (tokens // 128), axis=1)

    gains = [column(0), column(1)]
    loads["stash1"].wait()
    zg[1] = (stash_ref[1].astype(F32) * gains[1]).astype(BF16)
    loads["cot1"].wait()

    mirror_dy = send(cot_ref.at[1], md, m_s.at[0], m_r.at[0], mirror)
    mirror_z = send(zg.at[1], mz, m_s.at[1], m_r.at[1], mirror)

    def squares(wide):
        ones = jnp.ones((cols, 128), BF16)
        return dot((wide * wide).astype(BF16), ones, 0, 0)

    core_copies = []
    sums_wide = (two + 128, two, two)

    def core_send(g):
        away = pl.multiple_of((1 - core) * half, half)
        copy = send(
            part.at[g, pl.ds(away, half), : sums_wide[g]],
            r1.at[g, :, : sums_wide[g]],
            core_s.at[g],
            core_r.at[g],
            sibling,
        )
        copy.start()
        core_copies.append(copy)

    def partial_sums(g):
        if g == 0:
            loads["wd"].wait()
            part[0, :, :lat] = dot(zg[1], wd_ref[1], 0, 0).astype(BF16)
            loads["wu"].wait()
            part[0, :, lat:two] = dot(cot_ref[1], wu_ref[1], 0, 0).astype(BF16)
            loads["stash0"].wait()
            loads["fwd"].wait()
            lane = lax.broadcasted_iota(jnp.int32, (tokens, 128), 1)
            norms = squares(stash_ref[1].astype(F32))
            for index, array in enumerate((stash_ref.at[0], fwd_ref.at[0], fwd_ref.at[1])):
                norms = jnp.where(lane < 32 * (index + 1), norms, squares(array[...].astype(F32)))
            part[0, :, two:] = norms.astype(BF16)
        elif g == 1:
            zg[0] = (stash_ref[0].astype(F32) * gains[0]).astype(BF16)
            part[1, :, :lat] = dot(zg[0], wd_ref[0], 0, 0).astype(BF16)
            loads["cot0"].wait()
            part[1, :, lat:two] = dot(cot_ref[0], wu_ref[0], 0, 0).astype(BF16)
        else:
            for slot in range(2):
                rows = (fwd_ref[slot].astype(F32) * gains[slot]).astype(BF16)
                part[2, :, slot * lat : (slot + 1) * lat] = dot(rows, wd_ref[slot], 0, 0).astype(BF16)

    for g in range(3):
        partial_sums(g)
    pl.semaphore_wait(barrier, len(partners))
    mirror_dy.start()

    def rows_of(index):
        return pl.ds(pl.multiple_of(index * quarter, quarter), quarter)

    ya_copies, yb_copies = {}, {}

    def a_send(g, index, src, device):
        ya_copies[g, index] = send(src, ra.at[g, index], ya_s.at[g, index], ya_r.at[g, index], device)
        ya_copies[g, index].start()

    def b_send(g, index, src, device):
        spot = rb.at[g, index, :, : sums_wide[g] - lat]
        yb_copies[g, index] = send(src, spot, yb_s.at[g, index], yb_r.at[g, index], device)
        yb_copies[g, index].start()

    def core_sum(g):
        wide = sums_wide[g]
        core_copies[g].wait_recv()
        mine = part[g, pl.ds(pl.multiple_of(core * half, half), half), :wide].astype(F32)
        r1[g, :, :wide] = (mine + r1[g, :, :wide].astype(F32)).astype(BF16)
        a_send(g, 0, r1.at[g, rows_of(y2), :lat], side1)
        b_send(g, 0, r1.at[g, rows_of(y2), lat:wide], side3)
        a_send(g, 1, r1.at[g, rows_of(y1), :lat], side1)
        b_send(g, 1, r1.at[g, rows_of(y3), lat:wide], side3)

    def y_first(g):
        wide = sums_wide[g]
        ya_copies[g, 0].wait_recv()
        fa[g] = (r1[g, rows_of(y3), :lat].astype(F32) + ra[g, 0].astype(F32)).astype(BF16)
        a_send(g, 2, fa.at[g], side3)
        yb_copies[g, 0].wait_recv()
        fb[g, :, : wide - lat] = (
            r1[g, rows_of(y1), lat:wide].astype(F32) + rb[g, 0, :, : wide - lat].astype(F32)
        ).astype(BF16)
        b_send(g, 2, fb.at[g, :, : wide - lat], side1)

    x_copies = []

    def y_second(g):
        wide = sums_wide[g]
        mine = r1[g, rows_of(y), :wide].astype(F32)
        for index in (1, 2):
            ya_copies[g, index].wait_recv()
            yb_copies[g, index].wait_recv()
        h2[g, :, :lat] = (mine[:, :lat] + ra[g, 1].astype(F32) + ra[g, 2].astype(F32)).astype(BF16)
        h2[g, :, lat:wide] = (
            mine[:, lat:] + rb[g, 1, :, : wide - lat].astype(F32) + rb[g, 2, :, : wide - lat].astype(F32)
        ).astype(BF16)
        copy = send(
            h2.at[g, pl.ds(pl.multiple_of((1 - xh) * own, own), own), :wide],
            r3.at[g, :, :wide],
            x_s.at[g],
            x_r.at[g],
            across,
        )
        copy.start()
        x_copies.append(copy)

    base = pl.multiple_of(core * half + y * quarter + xh * own, own)

    def mean_sq(values):
        return jnp.sum(values * values, axis=1, keepdims=True) / lat

    mirror_rows = send(
        full.at[0, pl.ds(base, own), :two],
        full.at[3, pl.ds(base, own), :two],
        m_s.at[2],
        m_r.at[2],
        mirror,
    )
    gx_copies = {}
    widths = (two + 128, two + 128, two, two)

    def gx_send(g):
        spot = full.at[g, pl.ds(base, own), : widths[g]]
        gx_copies[g] = send(spot, spot, gx_s.at[g], gx_r.at[g], across)
        gx_copies[g].start()

    squared = []

    def own_rows(g):
        wide = sums_wide[g]
        x_copies[g].wait_recv()
        total = h2[g, pl.ds(pl.multiple_of(xh * own, own), own), :wide].astype(F32)
        total = total + r3[g, :, :wide].astype(F32)
        first, second = total[:, :lat], total[:, lat:two]
        if g == 0:
            for k in range(4):
                squared.append(total[:, two + 32 * k : two + 32 * k + 1] / features + EPS)
        square = squared[g]
        scale = lax.rsqrt(mean_sq(first) + EPS * square)
        unit = first * scale
        full[g, pl.ds(base, own), :lat] = unit.astype(BF16)
        if g < 2:
            mean = jnp.sum(second * unit, axis=1, keepdims=True) / lat
            cot = (scale * (second - unit * mean)).astype(BF16)
            full[g, pl.ds(base, own), lat:two] = cot
            pull = jnp.sum(cot.astype(F32) * first, axis=1, keepdims=True) / (features * square)
            full[g, pl.ds(base, own), two:] = jnp.broadcast_to(pull, (own, 128)).astype(BF16)
        else:
            scale = lax.rsqrt(mean_sq(second) + EPS * squared[3])
            full[g, pl.ds(base, own), lat:two] = (second * scale).astype(BF16)
        if g == 0:
            mirror_rows.start()
        gx_send(g)

    gy_copies, gc_copies = {}, {}

    def block_of(index):
        return pl.ds(pl.multiple_of(core * half + index * quarter, quarter), quarter)

    def gc_send(g, index, block):
        spot = full.at[g, block_of(block), : widths[g]]
        gc_copies[g, index] = send(spot, spot, gc_s.at[g, index], gc_r.at[g, index], sibling)
        gc_copies[g, index].start()

    def gy_start(g, index, spot, device):
        gy_copies[g, index] = send(spot, spot, gy_s.at[g, index], gy_r.at[g, index], device)
        gy_copies[g, index].start()

    def gy_send(g):
        gx_copies[g].wait_recv()
        spot = full.at[g, block_of(y), : widths[g]]
        gy_start(g, 0, spot, side1)
        gy_start(g, 1, spot, side3)
        gc_send(g, 0, y)

    def gy_pass(g):
        gy_copies[g, 1].wait_recv()
        gy_start(g, 2, full.at[g, block_of(y3), :lat], side1)
        gy_copies[g, 0].wait_recv()
        gy_start(g, 3, full.at[g, block_of(y1), lat : widths[g]], side3)
        gc_send(g, 1, y3)
        gc_send(g, 2, y1)

    def gy_last(g):
        gy_copies[g, 2].wait_recv()
        gy_copies[g, 3].wait_recv()
        gc_send(g, 3, y2)

    def gc_wait(g):
        for k in range(Y):
            gc_copies[g, k].wait_recv()

    ups = (pos < n_pipe - 1, pos > 0)

    def relay(index, slot, out, up):
        return send(rows_out.at[index], out.at[slot], n_s.at[index], n_r.at[index], above if up else below)

    relays = [
        relay(0, 1, bwd_out, True),
        relay(1, 0, bwd_out, False),
        relay(2, 0, fwd_out, True),
        relay(3, 1, fwd_out, False),
    ]

    def relay_start(index):
        @pl.when(ups[index % 2])
        def _():
            relays[index].start()

    mirror_gain = send(gsend, grecv, m_s.at[3], m_r.at[3], mirror)
    pick = jnp.where(lax.broadcasted_iota(jnp.int32, (8, 128), 1) == 0, 1.0, 0.0).astype(BF16)
    gain_parts = {}

    def results(g):
        gc_wait(g)
        if g == 2:
            for slot in range(2):
                branch = dot(wu_ref[slot], full[2, :, slot * lat : (slot + 1) * lat], 1, 1).astype(BF16)
                rows_out[2 + slot] = (fwd_ref[slot].astype(F32) + branch.astype(F32)).astype(BF16)
                relay_start(2 + slot)
            return
        slot = 1 - g
        scaled_cot = dot(wd_ref[slot], full[g, :, lat:two], 1, 1)
        wide = stash_ref[slot].astype(F32)
        pull = dot(pick, full[g, :, two:], 1, 1)[0:1, :]
        rows_out[g] = (
            cot_ref[slot].astype(F32) + scaled_cot * gains[slot] - wide * pull
        ).astype(BF16)
        relay_start(g)
        products = (wide * scaled_cot).astype(BF16)
        gain_parts[slot] = dot(jnp.ones((8, tokens), BF16), products, 1, 1)

    stages = (
        core_send,
        core_sum,
        y_first,
        y_second,
        own_rows,
        gy_send,
        gy_pass,
        gy_last,
        results,
    )
    for g in range(3):
        core_send(g)
    for step in range(1, len(stages) + 3):
        for g in range(4):
            stage = step - g - g // 3
            if 0 < stage < len(stages):
                if g < 3:
                    stages[stage](g)
                elif stage == 4:
                    mirror_rows.wait_recv()
                    mirror_z.start()
                    gx_send(3)
                elif 4 < stage < len(stages) - 1:
                    stages[stage](3)

    gsend[...] = gain_parts[1]
    mirror_gain.start()
    down_acc[...] = dot(zg[0], full[1, :, lat:two], 1, 0)
    up_acc[...] = dot(cot_ref[0], full[1, :, :lat], 1, 0)
    gc_wait(3)

    factor = tokens ** (-0.5)
    mirror_dy.wait_recv()
    up = up_acc[...] + dot(md[...], full[3, :, :lat], 1, 0)
    gu_out[...] = (up * factor).astype(BF16)
    mirror_z.wait_recv()
    down = down_acc[...] + dot(mz[...], full[3, :, lat:two], 1, 0)
    gd_out[...] = (down * factor).astype(BF16)
    mirror_gain.wait_recv()
    gg_out[...] = ((gain_parts[0] + grecv[...])[0:1, :] * factor).astype(BF16)

    def edge(here, first, second):
        @pl.when(here)
        def _():
            zg[0] = jnp.zeros((cols, tokens), BF16)
            one = pltpu.make_async_copy(zg.at[0], first, zero_sem.at[0])
            other = pltpu.make_async_copy(zg.at[0], second, zero_sem.at[1])
            one.start()
            other.start()
            one.wait()
            other.wait()

    edge(pos == 0, fwd_out.at[0], bwd_out.at[1])
    edge(pos == n_pipe - 1, fwd_out.at[1], bwd_out.at[0])

    for index in range(4):

        @pl.when(ups[index % 2])
        def _():
            relays[index].wait_send()

        @pl.when(ups[1 - index % 2])
        def _():
            relays[index].wait_recv()

    for copy in [
        mirror_dy,
        mirror_z,
        mirror_rows,
        mirror_gain,
        *core_copies,
        *ya_copies.values(),
        *yb_copies.values(),
        *x_copies,
        *gx_copies.values(),
        *gy_copies.values(),
        *gc_copies.values(),
    ]:
        copy.wait_send()


def place(*refs):
    count = (len(refs) - 2) // 3
    sources, targets, held = refs[:count], refs[count : 2 * count], refs[2 * count : 3 * count]
    arrive, leave = refs[3 * count :]
    copies = []
    for index in range(count):
        first = pltpu.make_async_copy(sources[index], held[index], arrive.at[index])
        second = pltpu.make_async_copy(held[index], targets[index], leave.at[index])
        first.start()
        copies.append((first, second))
    for first, second in copies:
        first.wait()
        second.start()
    for first, second in copies:
        second.wait()


def per_device(n_pipe, fwd_in, stash, cot_in, w_down, w_up, gain):
    tokens, cols = stash.shape[2:]
    lat = w_down.shape[3]
    wide = 2 * lat + 128
    half, quarter, own = tokens // 2, tokens // 8, tokens // 16
    vmem = pl.BlockSpec(memory_space=pltpu.VMEM)
    anywhere = pl.BlockSpec(memory_space=pl.ANY)
    dma = pltpu.SemaphoreType.DMA
    turned = lambda array: jnp.swapaxes(array[0], 1, 2)
    outs = pl.pallas_call(
        functools.partial(kernel, n_pipe),
        out_shape=(
            jax.ShapeDtypeStruct((2, cols, tokens), BF16),
            jax.ShapeDtypeStruct((2, cols, tokens), BF16),
            jax.ShapeDtypeStruct((cols, lat), BF16),
            jax.ShapeDtypeStruct((cols, lat), BF16),
            jax.ShapeDtypeStruct((1, cols), BF16),
        ),
        in_specs=[anywhere] * 5 + [vmem],
        out_specs=(anywhere, anywhere, vmem, vmem, vmem),
        scratch_shapes=[
            pltpu.VMEM((2, cols, tokens), BF16),
            pltpu.VMEM((2, cols, tokens), BF16),
            pltpu.VMEM((2, cols, tokens), BF16),
            pltpu.VMEM((2, cols, lat), BF16),
            pltpu.VMEM((2, cols, lat), BF16),
            pltpu.VMEM((3, tokens, wide), BF16),
            pltpu.VMEM((3, half, wide), BF16),
            pltpu.VMEM((3, 3, quarter, lat), BF16),
            pltpu.VMEM((3, 3, quarter, lat + 128), BF16),
            pltpu.VMEM((3, quarter, lat), BF16),
            pltpu.VMEM((3, quarter, lat + 128), BF16),
            pltpu.VMEM((3, quarter, wide), BF16),
            pltpu.VMEM((3, own, wide), BF16),
            pltpu.VMEM((4, tokens, wide), BF16),
            pltpu.VMEM((2, cols, tokens), BF16),
            pltpu.VMEM((cols, tokens), BF16),
            pltpu.VMEM((cols, tokens), BF16),
            pltpu.VMEM((8, cols), F32),
            pltpu.VMEM((8, cols), F32),
            pltpu.VMEM((4, cols, tokens), BF16),
            pltpu.VMEM((cols, lat), F32),
            pltpu.VMEM((cols, lat), F32),
            dma((7,)),
            dma((3,)),
            dma((3,)),
            dma((3, 3)),
            dma((3, 3)),
            dma((3, 3)),
            dma((3, 3)),
            dma((3,)),
            dma((3,)),
            dma((4,)),
            dma((4,)),
            dma((4, Y)),
            dma((4, Y)),
            dma((4, Y)),
            dma((4, Y)),
            dma((4,)),
            dma((4,)),
            dma((4,)),
            dma((4,)),
            dma((2,)),
        ],
        compiler_params=pltpu.CompilerParams(
            collective_id=0, has_side_effects=True, vmem_limit_bytes=56 * 1024 * 1024
        ),
    )(turned(fwd_in), turned(stash), turned(cot_in), w_down[0], turned(w_up), gain[0])
    fwd_next, bwd_next, grad_down, grad_up, grad_gain = pl.pallas_call(
        place,
        out_shape=tuple(jax.ShapeDtypeStruct(array.shape, array.dtype) for array in outs),
        in_specs=[anywhere] * 5,
        out_specs=(anywhere,) * 5,
        scratch_shapes=[pltpu.VMEM(array.shape, array.dtype) for array in outs] + [dma((5,)), dma((5,))],
        compiler_params=pltpu.CompilerParams(vmem_limit_bytes=56 * 1024 * 1024),
    )(*outs)
    return (
        jnp.swapaxes(fwd_next, 1, 2)[None],
        jnp.swapaxes(bwd_next, 1, 2)[None],
        grad_down[None],
        grad_up.T[None],
        grad_gain,
    )


def solution(mesh):
    placed = (
        P("pipe", None, None, "dp"),
        P("pipe", None, None, "dp"),
        P("pipe", None, None, "dp"),
        P("pipe", None, "dp", None),
        P("pipe", None, None, "dp"),
        P("pipe", None, "dp"),
    )
    return jax.shard_map(
        functools.partial(per_device, mesh.shape["pipe"]),
        mesh=mesh,
        in_specs=placed,
        out_specs=(
            P("pipe", None, None, "dp"),
            P("pipe", None, None, "dp"),
            P("pipe", "dp", None),
            P("pipe", None, "dp"),
            P("pipe", "dp"),
        ),
        check_vma=False,
    )
```

```python
import functools

import jax
import jax.numpy as jnp
from jax import lax
from jax.experimental import pallas as pl
from jax.experimental.pallas import tpu as pltpu
from jax.sharding import PartitionSpec as P

MESH = pl.DeviceIdType.MESH
EPS = 1e-06
BF16 = jnp.bfloat16
F32 = jnp.float32

Y, XH, CORE = 4, 2, 2


def dot(a, b, ca, cb):
    return lax.dot_general(a, b, (((ca,), (cb,)), ((), ())), preferred_element_type=F32)


def kernel(
    n_pipe,
    fwd_hbm,
    stash_hbm,
    cot_hbm,
    wd_hbm,
    wu_hbm,
    gain_ref,
    fwd_out,
    bwd_out,
    gd_out,
    gu_out,
    gg_out,
    fwd_ref,
    stash_ref,
    cot_ref,
    wd_ref,
    wu_ref,
    part,
    r1,
    r2,
    h2,
    r3,
    full,
    zg,
    mz,
    zx,
    md,
    gsend,
    grecv,
    rows_out,
    down_acc,
    gd_held,
    gu_held,
    in_sem,
    core_s,
    core_r,
    y_s,
    y_r,
    x_s,
    x_r,
    gx_s,
    gx_r,
    gy_s,
    gy_r,
    gc_s,
    gc_r,
    m_s,
    m_r,
    n_s,
    n_r,
    zero_sem,
    w_sem,
):
    pos = lax.axis_index("pipe")
    d = lax.axis_index("dp")
    cols, tokens = stash_ref.shape[1:]
    lat = wd_ref.shape[2]
    features = cols * Y * XH * CORE
    two = 2 * lat
    half, quarter, own = tokens // 2, tokens // 8, tokens // 16
    core = d % CORE
    xh = d // CORE % XH
    y = d // (CORE * XH)
    sibling = (pos, d + 1 - 2 * core)
    across = (pos, d + CORE * (1 - 2 * xh))
    ring = [(pos, (y + k) % Y * (CORE * XH) + d % (CORE * XH)) for k in range(1, Y)]
    mirror = (n_pipe - 1 - pos, d)
    beside = (pos + 1 - 2 * (pos % 2), d)
    opposite = (n_pipe - 2 - pos + 2 * (pos % 2), d)
    above = ((pos + 1) % n_pipe, d)
    below = ((pos + n_pipe - 1) % n_pipe, d)

    def send(src, dst, s_sem, r_sem, device):
        return pltpu.make_async_remote_copy(
            src_ref=src,
            dst_ref=dst,
            send_sem=s_sem,
            recv_sem=r_sem,
            device_id=device,
            device_id_type=MESH,
        )

    loads = {}
    for index, (name, src, dst) in enumerate(
        (
            ("cot1", cot_hbm.at[1], cot_ref.at[1]),
            ("stash1", stash_hbm.at[1], stash_ref.at[1]),
            ("wd", wd_hbm, wd_ref),
            ("wu", wu_hbm, wu_ref),
            ("stash0", stash_hbm.at[0], stash_ref.at[0]),
            ("cot0", cot_hbm.at[0], cot_ref.at[0]),
            ("fwd", fwd_hbm, fwd_ref),
        )
    ):
        loads[name] = pltpu.make_async_copy(src, dst, in_sem.at[index])
        loads[name].start()

    barrier = pltpu.get_barrier_semaphore()
    partners = [sibling, across, *ring, mirror, beside, opposite, above, below]
    for device in partners:
        pl.semaphore_signal(barrier, inc=1, device_id=device, device_id_type=MESH)

    def column(slot):
        wide = jnp.broadcast_to(gain_ref[slot : slot + 1, :], (128, cols)).T
        return jnp.concatenate([wide] * (tokens // 128), axis=1)

    gains = [column(0), column(1)]
    loads["stash1"].wait()
    zg[1] = (stash_ref[1].astype(F32) * gains[1]).astype(BF16)
    loads["cot1"].wait()

    mirror_dy = send(cot_ref.at[1], md, m_s.at[0], m_r.at[0], mirror)
    mirror_z_first = send(zg.at[1], zx, m_s.at[4], m_r.at[4], beside)
    mirror_z = send(zx, mz, m_s.at[1], m_r.at[1], opposite)

    def squares(wide):
        ones = jnp.ones((cols, 128), BF16)
        return dot((wide * wide).astype(BF16), ones, 0, 0)

    core_copies = []
    sums_wide = (two + 128, two, two)

    def core_send(g):
        away = pl.multiple_of((1 - core) * half, half)
        copy = send(
            part.at[g, pl.ds(away, half), : sums_wide[g]],
            r1.at[g, :, : sums_wide[g]],
            core_s.at[g],
            core_r.at[g],
            sibling,
        )
        copy.start()
        core_copies.append(copy)

    def partial_sums(g):
        if g == 0:
            loads["wd"].wait()
            part[0, :, :lat] = dot(zg[1], wd_ref[1], 0, 0).astype(BF16)
            loads["wu"].wait()
            part[0, :, lat:two] = dot(cot_ref[1], wu_ref[1], 0, 0).astype(BF16)
            loads["stash0"].wait()
            loads["fwd"].wait()
            lane = lax.broadcasted_iota(jnp.int32, (tokens, 128), 1)
            norms = squares(stash_ref[1].astype(F32))
            for index, array in enumerate((fwd_ref.at[0], fwd_ref.at[1], stash_ref.at[0])):
                norms = jnp.where(lane < 32 * (index + 1), norms, squares(array[...].astype(F32)))
            part[0, :, two:] = norms.astype(BF16)
        elif g == 2:
            zg[0] = (stash_ref[0].astype(F32) * gains[0]).astype(BF16)
            part[2, :, :lat] = dot(zg[0], wd_ref[0], 0, 0).astype(BF16)
            loads["cot0"].wait()
            part[2, :, lat:two] = dot(cot_ref[0], wu_ref[0], 0, 0).astype(BF16)
        else:
            for slot in range(2):
                rows = (fwd_ref[slot].astype(F32) * gains[slot]).astype(BF16)
                part[1, :, slot * lat : (slot + 1) * lat] = dot(rows, wd_ref[slot], 0, 0).astype(BF16)

    partial_sums(0)
    pl.semaphore_wait(barrier, len(partners))
    mirror_dy.start()
    mirror_z_first.start()
    core_send(0)
    for g in (1, 2):
        partial_sums(g)
        core_send(g)

    def rows_of(index):
        return pl.ds(pl.multiple_of(index * quarter, quarter), quarter)

    y_copies = {}

    def core_sum(g):
        wide = sums_wide[g]
        core_copies[g].wait_recv()
        mine = part[g, pl.ds(pl.multiple_of(core * half, half), half), :wide].astype(F32)
        r1[g, :, :wide] = (mine + r1[g, :, :wide].astype(F32)).astype(BF16)
        for k in range(Y - 1):
            y_copies[g, k] = send(
                r1.at[g, rows_of((y + k + 1) % Y), :wide],
                r2.at[g, k, :, :wide],
                y_s.at[g, k],
                y_r.at[g, k],
                ring[k],
            )
            y_copies[g, k].start()

    x_copies = []

    def y_sum(g):
        wide = sums_wide[g]
        total = r1[g, rows_of(y), :wide].astype(F32)
        for k in range(Y - 1):
            y_copies[g, k].wait_recv()
            total = total + r2[g, k, :, :wide].astype(F32)
        h2[g, :, :wide] = total.astype(BF16)
        copy = send(
            h2.at[g, pl.ds(pl.multiple_of((1 - xh) * own, own), own), :wide],
            r3.at[g, :, :wide],
            x_s.at[g],
            x_r.at[g],
            across,
        )
        copy.start()
        x_copies.append(copy)

    base = pl.multiple_of(core * half + y * quarter + xh * own, own)

    def mean_sq(values):
        return jnp.sum(values * values, axis=1, keepdims=True) / lat

    mirror_rows = send(
        full.at[0, pl.ds(base, own), :two],
        full.at[3, pl.ds(base, own), :two],
        m_s.at[2],
        m_r.at[2],
        mirror,
    )
    gx_copies = {}
    spans = ((lat, two + 128), (0, two), (lat, two + 128), (0, two + lat))

    def gx_send(g):
        spot = full.at[g, pl.ds(base, own), spans[g][0] : spans[g][1]]
        gx_copies[g] = send(spot, spot, gx_s.at[g], gx_r.at[g], across)
        gx_copies[g].start()

    squared = []

    def own_rows(g):
        wide = sums_wide[g]
        x_copies[g].wait_recv()
        total = h2[g, pl.ds(pl.multiple_of(xh * own, own), own), :wide].astype(F32)
        total = total + r3[g, :, :wide].astype(F32)
        first, second = total[:, :lat], total[:, lat:two]
        if g == 0:
            for k in range(4):
                squared.append(total[:, two + 32 * k : two + 32 * k + 1] / features + EPS)
        square = squared[(0, 1, 3)[g]]
        scale = lax.rsqrt(mean_sq(first) + EPS * square)
        unit = first * scale
        if g == 2:
            full[3, pl.ds(base, own), two : two + lat] = unit.astype(BF16)
        else:
            full[g, pl.ds(base, own), :lat] = unit.astype(BF16)
        if g == 1:
            scale = lax.rsqrt(mean_sq(second) + EPS * squared[2])
            full[g, pl.ds(base, own), lat:two] = (second * scale).astype(BF16)
        else:
            mean = jnp.sum(second * unit, axis=1, keepdims=True) / lat
            cot = (scale * (second - unit * mean)).astype(BF16)
            full[g, pl.ds(base, own), lat:two] = cot
            pull = jnp.sum(cot.astype(F32) * first, axis=1, keepdims=True) / (features * square)
            full[g, pl.ds(base, own), two : two + 128] = jnp.broadcast_to(pull, (own, 128)).astype(BF16)
        if g == 0:
            mirror_rows.start()
        gx_send(g)

    gy_copies, gc_copies = {}, {}

    def block_of(index):
        return pl.ds(pl.multiple_of(core * half + index * quarter, quarter), quarter)

    def gc_send(g, index, block):
        spot = full.at[g, block_of(block), spans[g][0] : spans[g][1]]
        gc_copies[g, index] = send(spot, spot, gc_s.at[g, index], gc_r.at[g, index], sibling)
        gc_copies[g, index].start()

    def gy_send(g):
        gx_copies[g].wait_recv()
        spot = full.at[g, block_of(y), spans[g][0] : spans[g][1]]
        for k in range(Y - 1):
            gy_copies[g, k] = send(spot, spot, gy_s.at[g, k], gy_r.at[g, k], ring[k])
            gy_copies[g, k].start()
        gc_send(g, 0, y)

    def gy_pass(g):
        for k in range(1, Y):
            gy_copies[g, k - 1].wait_recv()
            gc_send(g, k, (y + Y - k) % Y)

    def gc_wait(g):
        for k in range(Y):
            gc_copies[g, k].wait_recv()

    ups = (pos < n_pipe - 1, pos > 0)

    def relay(index, slot, out, up):
        return send(rows_out.at[index], out.at[slot], n_s.at[index], n_r.at[index], above if up else below)

    relays = [
        relay(0, 1, bwd_out, True),
        relay(1, 0, bwd_out, False),
        relay(2, 0, fwd_out, True),
        relay(3, 1, fwd_out, False),
    ]

    def relay_start(index):
        @pl.when(ups[index % 2])
        def _():
            relays[index].start()

    mirror_gain = send(gsend, grecv, m_s.at[3], m_r.at[3], mirror)
    pick = jnp.where(lax.broadcasted_iota(jnp.int32, (8, 128), 1) == 0, 1.0, 0.0).astype(BF16)
    gain_parts = {}

    def results(g):
        gc_wait(g)
        if g == 1:
            for slot in range(2):
                branch = dot(wu_ref[slot], full[1, :, slot * lat : (slot + 1) * lat], 1, 1).astype(BF16)
                rows_out[2 + slot] = (fwd_ref[slot].astype(F32) + branch.astype(F32)).astype(BF16)
                relay_start(2 + slot)
            return
        slot = 1 - g // 2
        scaled_cot = dot(wd_ref[slot], full[g, :, lat:two], 1, 1)
        wide = stash_ref[slot].astype(F32)
        pull = dot(pick, full[g, :, two : two + 128], 1, 1)[0:1, :]
        rows_out[1 - slot] = (
            cot_ref[slot].astype(F32) + scaled_cot * gains[slot] - wide * pull
        ).astype(BF16)
        relay_start(1 - slot)
        products = (wide * scaled_cot).astype(BF16)
        gain_parts[slot] = dot(jnp.ones((8, tokens), BF16), products, 1, 1)

    core_sum(0)
    core_sum(1)
    y_sum(0)
    core_sum(2)
    y_sum(1)
    own_rows(0)
    y_sum(2)
    for stage in (own_rows, gy_send, gy_pass):
        for g in range(3):
            if g or stage is not own_rows:
                stage(g)
    mirror_rows.wait_recv()
    mirror_z_first.wait_recv()
    mirror_z.start()
    gx_send(3)
    results(0)
    gy_send(3)
    results(1)
    gy_pass(3)
    results(2)
    gsend[...] = gain_parts[1]
    mirror_gain.start()
    down_acc[...] = dot(zg[0], full[2, :, lat:two], 1, 0)
    gc_wait(3)

    factor = tokens ** (-0.5)
    mirror_dy.wait_recv()
    up = dot(cot_ref[0], full[3, :, two : two + lat], 1, 0) + dot(md[...], full[3, :, :lat], 1, 0)
    gu_held[...] = (up * factor).astype(BF16)
    leaving = [pltpu.make_async_copy(gu_held, gu_out, w_sem.at[0])]
    leaving[0].start()
    mirror_z.wait_recv()
    for index in range(2):
        rows = pl.ds(index * (cols // 2), cols // 2)
        down = down_acc[rows, :] + dot(mz[rows, :], full[3, :, lat:two], 1, 0)
        gd_held[rows, :] = (down * factor).astype(BF16)
        leaving.append(pltpu.make_async_copy(gd_held.at[rows], gd_out.at[rows], w_sem.at[index + 1]))
        leaving[-1].start()
    mirror_gain.wait_recv()
    gg_out[...] = ((gain_parts[0] + grecv[...])[0:1, :] * factor).astype(BF16)

    def edge(here, first, second):
        @pl.when(here)
        def _():
            zg[0] = jnp.zeros((cols, tokens), BF16)
            one = pltpu.make_async_copy(zg.at[0], first, zero_sem.at[0])
            other = pltpu.make_async_copy(zg.at[0], second, zero_sem.at[1])
            one.start()
            other.start()
            one.wait()
            other.wait()

    edge(pos == 0, fwd_out.at[0], bwd_out.at[1])
    edge(pos == n_pipe - 1, fwd_out.at[1], bwd_out.at[0])

    for copy in leaving:
        copy.wait()
    for index in range(4):

        @pl.when(ups[index % 2])
        def _():
            relays[index].wait_send()

        @pl.when(ups[1 - index % 2])
        def _():
            relays[index].wait_recv()

    for copy in [
        mirror_dy,
        mirror_z,
        mirror_z_first,
        mirror_rows,
        mirror_gain,
        *core_copies,
        *y_copies.values(),
        *x_copies,
        *gx_copies.values(),
        *gy_copies.values(),
        *gc_copies.values(),
    ]:
        copy.wait_send()


def place(*refs):
    count = (len(refs) - 2) // 3
    sources, targets, held = refs[:count], refs[count : 2 * count], refs[2 * count : 3 * count]
    arrive, leave = refs[3 * count :]
    copies = []
    for index in range(count):
        first = pltpu.make_async_copy(sources[index], held[index], arrive.at[index])
        second = pltpu.make_async_copy(held[index], targets[index], leave.at[index])
        first.start()
        copies.append((first, second))
    for first, second in copies:
        first.wait()
        second.start()
    for first, second in copies:
        second.wait()


def per_device(n_pipe, fwd_in, stash, cot_in, w_down, w_up, gain):
    tokens, cols = stash.shape[2:]
    lat = w_down.shape[3]
    wide = 2 * lat + 128
    half, quarter, own = tokens // 2, tokens // 8, tokens // 16
    vmem = pl.BlockSpec(memory_space=pltpu.VMEM)
    anywhere = pl.BlockSpec(memory_space=pl.ANY)
    dma = pltpu.SemaphoreType.DMA
    turned = lambda array: jnp.swapaxes(array[0], 1, 2)
    outs = pl.pallas_call(
        functools.partial(kernel, n_pipe),
        out_shape=(
            jax.ShapeDtypeStruct((2, cols, tokens), BF16),
            jax.ShapeDtypeStruct((2, cols, tokens), BF16),
            jax.ShapeDtypeStruct((cols, lat), BF16),
            jax.ShapeDtypeStruct((cols, lat), BF16),
            jax.ShapeDtypeStruct((1, cols), BF16),
        ),
        in_specs=[anywhere] * 5 + [vmem],
        out_specs=(anywhere,) * 4 + (vmem,),
        scratch_shapes=[
            pltpu.VMEM((2, cols, tokens), BF16),
            pltpu.VMEM((2, cols, tokens), BF16),
            pltpu.VMEM((2, cols, tokens), BF16),
            pltpu.VMEM((2, cols, lat), BF16),
            pltpu.VMEM((2, cols, lat), BF16),
            pltpu.VMEM((3, tokens, wide), BF16),
            pltpu.VMEM((3, half, wide), BF16),
            pltpu.VMEM((3, Y - 1, quarter, wide), BF16),
            pltpu.VMEM((3, quarter, wide), BF16),
            pltpu.VMEM((3, own, wide), BF16),
            pltpu.VMEM((4, tokens, 3 * lat), BF16),
            pltpu.VMEM((2, cols, tokens), BF16),
            pltpu.VMEM((cols, tokens), BF16),
            pltpu.VMEM((cols, tokens), BF16),
            pltpu.VMEM((cols, tokens), BF16),
            pltpu.VMEM((8, cols), F32),
            pltpu.VMEM((8, cols), F32),
            pltpu.VMEM((4, cols, tokens), BF16),
            pltpu.VMEM((cols, lat), F32),
            pltpu.VMEM((cols, lat), BF16),
            pltpu.VMEM((cols, lat), BF16),
            dma((7,)),
            dma((3,)),
            dma((3,)),
            dma((3, Y - 1)),
            dma((3, Y - 1)),
            dma((3,)),
            dma((3,)),
            dma((4,)),
            dma((4,)),
            dma((4, Y - 1)),
            dma((4, Y - 1)),
            dma((4, Y)),
            dma((4, Y)),
            dma((5,)),
            dma((5,)),
            dma((4,)),
            dma((4,)),
            dma((2,)),
            dma((3,)),
        ],
        compiler_params=pltpu.CompilerParams(
            collective_id=0, has_side_effects=True, vmem_limit_bytes=56 * 1024 * 1024
        ),
    )(turned(fwd_in), turned(stash), turned(cot_in), w_down[0], turned(w_up), gain[0])
    fwd_next, bwd_next, grad_down, grad_up, grad_gain = pl.pallas_call(
        place,
        out_shape=tuple(jax.ShapeDtypeStruct(array.shape, array.dtype) for array in outs),
        in_specs=[anywhere] * 5,
        out_specs=(anywhere,) * 5,
        scratch_shapes=[pltpu.VMEM(array.shape, array.dtype) for array in outs] + [dma((5,)), dma((5,))],
        compiler_params=pltpu.CompilerParams(vmem_limit_bytes=56 * 1024 * 1024),
    )(*outs)
    return (
        jnp.swapaxes(fwd_next, 1, 2)[None],
        jnp.swapaxes(bwd_next, 1, 2)[None],
        grad_down[None],
        grad_up.T[None],
        grad_gain,
    )


def solution(mesh):
    placed = (
        P("pipe", None, None, "dp"),
        P("pipe", None, None, "dp"),
        P("pipe", None, None, "dp"),
        P("pipe", None, "dp", None),
        P("pipe", None, None, "dp"),
        P("pipe", None, "dp"),
    )
    return jax.shard_map(
        functools.partial(per_device, mesh.shape["pipe"]),
        mesh=mesh,
        in_specs=placed,
        out_specs=(
            P("pipe", None, None, "dp"),
            P("pipe", None, None, "dp"),
            P("pipe", "dp", None),
            P("pipe", None, "dp"),
            P("pipe", "dp"),
        ),
        check_vma=False,
    )
```

```python
import functools

import jax
import jax.numpy as jnp
from jax import lax
from jax.experimental import pallas as pl
from jax.experimental.pallas import tpu as pltpu
from jax.sharding import PartitionSpec as P

MESH = pl.DeviceIdType.MESH
EPS = 1e-06
BF16 = jnp.bfloat16
F32 = jnp.float32

Y, XH, CORE = 4, 2, 2


def dot(a, b, ca, cb):
    return lax.dot_general(a, b, (((ca,), (cb,)), ((), ())), preferred_element_type=F32)


def kernel(
    n_pipe,
    fwd_hbm,
    stash_hbm,
    cot_hbm,
    wd_hbm,
    wu_hbm,
    gain_ref,
    fwd_out,
    bwd_out,
    gd_out,
    gu_out,
    gg_out,
    fwd_ref,
    stash_ref,
    cot_ref,
    wd_ref,
    wu_ref,
    part,
    r1,
    r2,
    h2,
    r3,
    full,
    zg,
    mz,
    zx,
    md,
    gsend,
    grecv,
    rows_out,
    down_acc,
    gd_held,
    gu_held,
    in_sem,
    core_s,
    core_r,
    y_s,
    y_r,
    x_s,
    x_r,
    gx_s,
    gx_r,
    gy_s,
    gy_r,
    gc_s,
    gc_r,
    m_s,
    m_r,
    n_s,
    n_r,
    zero_sem,
    w_sem,
):
    pos = lax.axis_index("pipe")
    d = lax.axis_index("dp")
    cols, tokens = stash_ref.shape[1:]
    lat = wd_ref.shape[2]
    features = cols * Y * XH * CORE
    two = 2 * lat
    half, quarter, own = tokens // 2, tokens // 8, tokens // 16
    core = d % CORE
    xh = d // CORE % XH
    y = d // (CORE * XH)
    sibling = (pos, d + 1 - 2 * core)
    across = (pos, d + CORE * (1 - 2 * xh))
    ring = [(pos, (y + k) % Y * (CORE * XH) + d % (CORE * XH)) for k in range(1, Y)]
    mirror = (n_pipe - 1 - pos, d)
    beside = (pos + 1 - 2 * (pos % 2), d)
    opposite = (n_pipe - 2 - pos + 2 * (pos % 2), d)
    above = ((pos + 1) % n_pipe, d)
    below = ((pos + n_pipe - 1) % n_pipe, d)

    def send(src, dst, s_sem, r_sem, device):
        return pltpu.make_async_remote_copy(
            src_ref=src,
            dst_ref=dst,
            send_sem=s_sem,
            recv_sem=r_sem,
            device_id=device,
            device_id_type=MESH,
        )

    loads = {}
    for index, (name, src, dst) in enumerate(
        (
            ("cot1", cot_hbm.at[1], cot_ref.at[1]),
            ("stash1", stash_hbm.at[1], stash_ref.at[1]),
            ("wd", wd_hbm, wd_ref),
            ("wu", wu_hbm, wu_ref),
            ("stash0", stash_hbm.at[0], stash_ref.at[0]),
            ("cot0", cot_hbm.at[0], cot_ref.at[0]),
            ("fwd", fwd_hbm, fwd_ref),
        )
    ):
        loads[name] = pltpu.make_async_copy(src, dst, in_sem.at[index])
        loads[name].start()

    barrier = pltpu.get_barrier_semaphore()
    partners = [sibling, across, *ring, mirror, beside, opposite, above, below]
    for device in partners:
        pl.semaphore_signal(barrier, inc=1, device_id=device, device_id_type=MESH)

    def column(slot):
        wide = jnp.broadcast_to(gain_ref[slot : slot + 1, :], (128, cols)).T
        return jnp.concatenate([wide] * (tokens // 128), axis=1)

    gains = [column(0), column(1)]
    loads["stash1"].wait()
    zg[1] = (stash_ref[1].astype(F32) * gains[1]).astype(BF16)
    loads["cot1"].wait()

    mirror_dy = send(cot_ref.at[1], md, m_s.at[0], m_r.at[0], mirror)
    mirror_z_first = send(zg.at[1], zx, m_s.at[4], m_r.at[4], beside)
    mirror_z = send(zx, mz, m_s.at[1], m_r.at[1], opposite)

    def squares(wide):
        ones = jnp.ones((cols, 128), BF16)
        return dot((wide * wide).astype(BF16), ones, 0, 0)

    core_copies = []
    sums_wide = (two + 128, two, two)

    def core_send(g):
        away = pl.multiple_of((1 - core) * half, half)
        copy = send(
            part.at[g, pl.ds(away, half), : sums_wide[g]],
            r1.at[g, :, : sums_wide[g]],
            core_s.at[g],
            core_r.at[g],
            sibling,
        )
        copy.start()
        core_copies.append(copy)

    def partial_sums(g):
        if g == 0:
            loads["wd"].wait()
            part[0, :, :lat] = dot(zg[1], wd_ref[1], 0, 0).astype(BF16)
            loads["wu"].wait()
            part[0, :, lat:two] = dot(cot_ref[1], wu_ref[1], 0, 0).astype(BF16)
            loads["stash0"].wait()
            loads["fwd"].wait()
            lane = lax.broadcasted_iota(jnp.int32, (tokens, 128), 1)
            norms = squares(stash_ref[1].astype(F32))
            for index, array in enumerate((fwd_ref.at[0], fwd_ref.at[1], stash_ref.at[0])):
                norms = jnp.where(lane < 32 * (index + 1), norms, squares(array[...].astype(F32)))
            part[0, :, two:] = norms.astype(BF16)
        elif g == 2:
            zg[0] = (stash_ref[0].astype(F32) * gains[0]).astype(BF16)
            part[2, :, :lat] = dot(zg[0], wd_ref[0], 0, 0).astype(BF16)
            loads["cot0"].wait()
            part[2, :, lat:two] = dot(cot_ref[0], wu_ref[0], 0, 0).astype(BF16)
        else:
            for slot in range(2):
                rows = (fwd_ref[slot].astype(F32) * gains[slot]).astype(BF16)
                part[1, :, slot * lat : (slot + 1) * lat] = dot(rows, wd_ref[slot], 0, 0).astype(BF16)

    partial_sums(0)
    pl.semaphore_wait(barrier, len(partners))
    mirror_dy.start()
    mirror_z_first.start()
    core_send(0)
    for g in (1, 2):
        partial_sums(g)
        core_send(g)

    def rows_of(index):
        return pl.ds(pl.multiple_of(index * quarter, quarter), quarter)

    y_copies = {}

    def core_sum(g):
        wide = sums_wide[g]
        core_copies[g].wait_recv()
        mine = part[g, pl.ds(pl.multiple_of(core * half, half), half), :wide].astype(F32)
        r1[g, :, :wide] = (mine + r1[g, :, :wide].astype(F32)).astype(BF16)
        for k in range(Y - 1):
            y_copies[g, k] = send(
                r1.at[g, rows_of((y + k + 1) % Y), :wide],
                r2.at[g, k, :, :wide],
                y_s.at[g, k],
                y_r.at[g, k],
                ring[k],
            )
            y_copies[g, k].start()

    x_copies = []

    def y_sum(g):
        wide = sums_wide[g]
        total = r1[g, rows_of(y), :wide].astype(F32)
        for k in range(Y - 1):
            y_copies[g, k].wait_recv()
            total = total + r2[g, k, :, :wide].astype(F32)
        h2[g, :, :wide] = total.astype(BF16)
        copy = send(
            h2.at[g, pl.ds(pl.multiple_of((1 - xh) * own, own), own), :wide],
            r3.at[g, :, :wide],
            x_s.at[g],
            x_r.at[g],
            across,
        )
        copy.start()
        x_copies.append(copy)

    base = pl.multiple_of(core * half + y * quarter + xh * own, own)

    def mean_sq(values):
        return jnp.sum(values * values, axis=1, keepdims=True) / lat

    mirror_rows = send(
        full.at[0, pl.ds(base, own), :two],
        full.at[3, pl.ds(base, own), :two],
        m_s.at[2],
        m_r.at[2],
        mirror,
    )
    gx_copies = {}
    spans = ((lat, two + 128), (0, two), (lat, two + 128), (0, two + lat))

    def gx_send(g):
        spot = full.at[g, pl.ds(base, own), spans[g][0] : spans[g][1]]
        gx_copies[g] = send(spot, spot, gx_s.at[g], gx_r.at[g], across)
        gx_copies[g].start()

    squared = []

    def own_rows(g):
        wide = sums_wide[g]
        x_copies[g].wait_recv()
        total = h2[g, pl.ds(pl.multiple_of(xh * own, own), own), :wide].astype(F32)
        total = total + r3[g, :, :wide].astype(F32)
        first, second = total[:, :lat], total[:, lat:two]
        if g == 0:
            for k in range(4):
                squared.append(total[:, two + 32 * k : two + 32 * k + 1] / features + EPS)
        square = squared[(0, 1, 3)[g]]
        scale = lax.rsqrt(mean_sq(first) + EPS * square)
        unit = first * scale
        if g == 2:
            full[3, pl.ds(base, own), two : two + lat] = unit.astype(BF16)
        else:
            full[g, pl.ds(base, own), :lat] = unit.astype(BF16)
        if g == 1:
            scale = lax.rsqrt(mean_sq(second) + EPS * squared[2])
            full[g, pl.ds(base, own), lat:two] = (second * scale).astype(BF16)
        else:
            mean = jnp.sum(second * unit, axis=1, keepdims=True) / lat
            cot = (scale * (second - unit * mean)).astype(BF16)
            full[g, pl.ds(base, own), lat:two] = cot
            pull = jnp.sum(cot.astype(F32) * first, axis=1, keepdims=True) / (features * square)
            full[g, pl.ds(base, own), two : two + 128] = jnp.broadcast_to(pull, (own, 128)).astype(BF16)
        if g == 0:
            mirror_rows.start()
        gx_send(g)

    gy_copies, gc_copies = {}, {}

    def block_of(index):
        return pl.ds(pl.multiple_of(core * half + index * quarter, quarter), quarter)

    def gc_send(g, index, block):
        spot = full.at[g, block_of(block), spans[g][0] : spans[g][1]]
        gc_copies[g, index] = send(spot, spot, gc_s.at[g, index], gc_r.at[g, index], sibling)
        gc_copies[g, index].start()

    def gy_send(g):
        gx_copies[g].wait_recv()
        spot = full.at[g, block_of(y), spans[g][0] : spans[g][1]]
        for k in range(Y - 1):
            gy_copies[g, k] = send(spot, spot, gy_s.at[g, k], gy_r.at[g, k], ring[k])
            gy_copies[g, k].start()
        gc_send(g, 0, y)

    def gy_pass(g):
        for k in range(1, Y):
            gy_copies[g, k - 1].wait_recv()
            gc_send(g, k, (y + Y - k) % Y)

    def gc_wait(g):
        for k in range(Y):
            gc_copies[g, k].wait_recv()

    ups = (pos < n_pipe - 1, pos > 0)

    def relay(index, slot, out, up):
        return send(rows_out.at[index], out.at[slot], n_s.at[index], n_r.at[index], above if up else below)

    relays = [
        relay(0, 1, bwd_out, True),
        relay(1, 0, bwd_out, False),
        relay(2, 0, fwd_out, True),
        relay(3, 1, fwd_out, False),
    ]

    def relay_start(index):
        @pl.when(ups[index % 2])
        def _():
            relays[index].start()

    mirror_gain = send(gsend, grecv, m_s.at[3], m_r.at[3], mirror)
    pick = jnp.where(lax.broadcasted_iota(jnp.int32, (8, 128), 1) == 0, 1.0, 0.0).astype(BF16)
    gain_parts = {}

    def results(g):
        gc_wait(g)
        if g == 1:
            for slot in range(2):
                branch = dot(wu_ref[slot], full[1, :, slot * lat : (slot + 1) * lat], 1, 1).astype(BF16)
                rows_out[2 + slot] = (fwd_ref[slot].astype(F32) + branch.astype(F32)).astype(BF16)
                relay_start(2 + slot)
            return
        slot = 1 - g // 2
        scaled_cot = dot(wd_ref[slot], full[g, :, lat:two], 1, 1)
        wide = stash_ref[slot].astype(F32)
        pull = dot(pick, full[g, :, two : two + 128], 1, 1)[0:1, :]
        rows_out[1 - slot] = (
            cot_ref[slot].astype(F32) + scaled_cot * gains[slot] - wide * pull
        ).astype(BF16)
        relay_start(1 - slot)
        products = (wide * scaled_cot).astype(BF16)
        gain_parts[slot] = dot(jnp.ones((8, tokens), BF16), products, 1, 1)

    core_sum(0)
    core_sum(1)
    y_sum(0)
    core_sum(2)
    y_sum(1)
    own_rows(0)
    y_sum(2)
    for stage in (own_rows, gy_send, gy_pass):
        for g in range(3):
            if g or stage is not own_rows:
                stage(g)
    mirror_rows.wait_recv()
    mirror_z_first.wait_recv()
    mirror_z.start()
    gx_send(3)
    results(0)
    gy_send(3)
    results(1)
    gy_pass(3)
    results(2)
    gsend[...] = gain_parts[1]
    mirror_gain.start()
    down_acc[...] = dot(zg[0], full[2, :, lat:two], 1, 0)
    gc_wait(3)

    factor = tokens ** (-0.5)
    mirror_dy.wait_recv()
    up = dot(cot_ref[0], full[3, :, two : two + lat], 1, 0) + dot(md[...], full[3, :, :lat], 1, 0)
    gu_held[...] = (up * factor).astype(BF16)
    leaving = [pltpu.make_async_copy(gu_held, gu_out, w_sem.at[0])]
    leaving[0].start()
    mirror_z.wait_recv()
    for index in range(2):
        rows = pl.ds(index * (cols // 2), cols // 2)
        down = down_acc[rows, :] + dot(mz[rows, :], full[3, :, lat:two], 1, 0)
        gd_held[rows, :] = (down * factor).astype(BF16)
        leaving.append(pltpu.make_async_copy(gd_held.at[rows], gd_out.at[rows], w_sem.at[index + 1]))
        leaving[-1].start()
    mirror_gain.wait_recv()
    gg_out[...] = ((gain_parts[0] + grecv[...])[0:1, :] * factor).astype(BF16)

    def edge(here, first, second):
        @pl.when(here)
        def _():
            zg[0] = jnp.zeros((cols, tokens), BF16)
            one = pltpu.make_async_copy(zg.at[0], first, zero_sem.at[0])
            other = pltpu.make_async_copy(zg.at[0], second, zero_sem.at[1])
            one.start()
            other.start()
            one.wait()
            other.wait()

    edge(pos == 0, fwd_out.at[0], bwd_out.at[1])
    edge(pos == n_pipe - 1, fwd_out.at[1], bwd_out.at[0])

    for copy in leaving:
        copy.wait()
    for index in range(4):

        @pl.when(ups[index % 2])
        def _():
            relays[index].wait_send()

        @pl.when(ups[1 - index % 2])
        def _():
            relays[index].wait_recv()

    for copy in [
        mirror_dy,
        mirror_z,
        mirror_z_first,
        mirror_rows,
        mirror_gain,
        *core_copies,
        *y_copies.values(),
        *x_copies,
        *gx_copies.values(),
        *gy_copies.values(),
        *gc_copies.values(),
    ]:
        copy.wait_send()


def place(*refs):
    count = len(refs) // 2
    sources, targets, sems = refs[:count], refs[count:-1], refs[-1]
    copies = [
        pltpu.make_async_copy(sources[index], targets[index], sems.at[index]) for index in range(count)
    ]
    for copy in copies:
        copy.start()
    for copy in copies:
        copy.wait()


def per_device(n_pipe, fwd_in, stash, cot_in, w_down, w_up, gain):
    tokens, cols = stash.shape[2:]
    lat = w_down.shape[3]
    wide = 2 * lat + 128
    half, quarter, own = tokens // 2, tokens // 8, tokens // 16
    vmem = pl.BlockSpec(memory_space=pltpu.VMEM)
    anywhere = pl.BlockSpec(memory_space=pl.ANY)
    dma = pltpu.SemaphoreType.DMA
    turned = lambda array: jnp.swapaxes(array[0], 1, 2)
    outs = pl.pallas_call(
        functools.partial(kernel, n_pipe),
        out_shape=(
            jax.ShapeDtypeStruct((2, cols, tokens), BF16),
            jax.ShapeDtypeStruct((2, cols, tokens), BF16),
            jax.ShapeDtypeStruct((cols, lat), BF16),
            jax.ShapeDtypeStruct((cols, lat), BF16),
            jax.ShapeDtypeStruct((1, cols), BF16),
        ),
        in_specs=[anywhere] * 5 + [vmem],
        out_specs=(anywhere,) * 4 + (vmem,),
        scratch_shapes=[
            pltpu.VMEM((2, cols, tokens), BF16),
            pltpu.VMEM((2, cols, tokens), BF16),
            pltpu.VMEM((2, cols, tokens), BF16),
            pltpu.VMEM((2, cols, lat), BF16),
            pltpu.VMEM((2, cols, lat), BF16),
            pltpu.VMEM((3, tokens, wide), BF16),
            pltpu.VMEM((3, half, wide), BF16),
            pltpu.VMEM((3, Y - 1, quarter, wide), BF16),
            pltpu.VMEM((3, quarter, wide), BF16),
            pltpu.VMEM((3, own, wide), BF16),
            pltpu.VMEM((4, tokens, 3 * lat), BF16),
            pltpu.VMEM((2, cols, tokens), BF16),
            pltpu.VMEM((cols, tokens), BF16),
            pltpu.VMEM((cols, tokens), BF16),
            pltpu.VMEM((cols, tokens), BF16),
            pltpu.VMEM((8, cols), F32),
            pltpu.VMEM((8, cols), F32),
            pltpu.VMEM((4, cols, tokens), BF16),
            pltpu.VMEM((cols, lat), F32),
            pltpu.VMEM((cols, lat), BF16),
            pltpu.VMEM((cols, lat), BF16),
            dma((7,)),
            dma((3,)),
            dma((3,)),
            dma((3, Y - 1)),
            dma((3, Y - 1)),
            dma((3,)),
            dma((3,)),
            dma((4,)),
            dma((4,)),
            dma((4, Y - 1)),
            dma((4, Y - 1)),
            dma((4, Y)),
            dma((4, Y)),
            dma((5,)),
            dma((5,)),
            dma((4,)),
            dma((4,)),
            dma((2,)),
            dma((3,)),
        ],
        compiler_params=pltpu.CompilerParams(
            collective_id=0, has_side_effects=True, vmem_limit_bytes=52 * 1024 * 1024
        ),
    )(turned(fwd_in), turned(stash), turned(cot_in), w_down[0], turned(w_up), gain[0])
    fwd_next, bwd_next, grad_down, grad_up, grad_gain = pl.pallas_call(
        place,
        out_shape=tuple(jax.ShapeDtypeStruct(array.shape, array.dtype) for array in outs),
        in_specs=[vmem] * 5,
        out_specs=(anywhere,) * 5,
        scratch_shapes=[dma((5,))],
        compiler_params=pltpu.CompilerParams(vmem_limit_bytes=16 * 1024 * 1024),
    )(*outs)
    return (
        jnp.swapaxes(fwd_next, 1, 2)[None],
        jnp.swapaxes(bwd_next, 1, 2)[None],
        grad_down[None],
        grad_up.T[None],
        grad_gain,
    )


def solution(mesh):
    placed = (
        P("pipe", None, None, "dp"),
        P("pipe", None, None, "dp"),
        P("pipe", None, None, "dp"),
        P("pipe", None, "dp", None),
        P("pipe", None, None, "dp"),
        P("pipe", None, "dp"),
    )
    return jax.shard_map(
        functools.partial(per_device, mesh.shape["pipe"]),
        mesh=mesh,
        in_specs=placed,
        out_specs=(
            P("pipe", None, None, "dp"),
            P("pipe", None, None, "dp"),
            P("pipe", "dp", None),
            P("pipe", None, "dp"),
            P("pipe", "dp"),
        ),
        check_vma=False,
    )
```

```python
import functools

import jax
import jax.numpy as jnp
from jax import lax
from jax.experimental import pallas as pl
from jax.experimental.pallas import tpu as pltpu
from jax.sharding import PartitionSpec as P

MESH = pl.DeviceIdType.MESH
EPS = 1e-06
BF16 = jnp.bfloat16
F32 = jnp.float32

Y, XH, CORE = 4, 2, 2


def dot(a, b, ca, cb):
    return lax.dot_general(a, b, (((ca,), (cb,)), ((), ())), preferred_element_type=F32)


def kernel(
    n_pipe,
    fwd_hbm,
    stash_hbm,
    cot_hbm,
    wd_hbm,
    wu_hbm,
    gain_ref,
    fwd_out,
    bwd_out,
    gd_out,
    gu_out,
    gg_out,
    fwd_ref,
    stash_ref,
    cot_ref,
    wd_ref,
    wu_ref,
    part,
    r1,
    r2,
    h2,
    r3,
    full,
    zg,
    mz,
    zx,
    md,
    gsend,
    grecv,
    rows_out,
    down_acc,
    in_sem,
    core_s,
    core_r,
    y_s,
    y_r,
    x_s,
    x_r,
    gx_s,
    gx_r,
    gy_s,
    gy_r,
    gc_s,
    gc_r,
    m_s,
    m_r,
    n_s,
    n_r,
    zero_sem,
):
    pos = lax.axis_index("pipe")
    d = lax.axis_index("dp")
    cols, tokens = stash_ref.shape[1:]
    lat = wd_ref.shape[2]
    features = cols * Y * XH * CORE
    two = 2 * lat
    half, quarter, own = tokens // 2, tokens // 8, tokens // 16
    core = d % CORE
    xh = d // CORE % XH
    y = d // (CORE * XH)
    sibling = (pos, d + 1 - 2 * core)
    across = (pos, d + CORE * (1 - 2 * xh))
    ring = [(pos, (y + k) % Y * (CORE * XH) + d % (CORE * XH)) for k in range(1, Y)]
    mirror = (n_pipe - 1 - pos, d)
    beside = (pos + 1 - 2 * (pos % 2), d)
    opposite = (n_pipe - 2 - pos + 2 * (pos % 2), d)
    above = ((pos + 1) % n_pipe, d)
    below = ((pos + n_pipe - 1) % n_pipe, d)

    def send(src, dst, s_sem, r_sem, device):
        return pltpu.make_async_remote_copy(
            src_ref=src,
            dst_ref=dst,
            send_sem=s_sem,
            recv_sem=r_sem,
            device_id=device,
            device_id_type=MESH,
        )

    loads = {}
    for index, (name, src, dst) in enumerate(
        (
            ("cot1", cot_hbm.at[1], cot_ref.at[1]),
            ("stash1", stash_hbm.at[1], stash_ref.at[1]),
            ("wd", wd_hbm, wd_ref),
            ("wu", wu_hbm, wu_ref),
            ("stash0", stash_hbm.at[0], stash_ref.at[0]),
            ("cot0", cot_hbm.at[0], cot_ref.at[0]),
            ("fwd", fwd_hbm, fwd_ref),
        )
    ):
        loads[name] = pltpu.make_async_copy(src, dst, in_sem.at[index])
        loads[name].start()

    barrier = pltpu.get_barrier_semaphore()
    partners = [sibling, across, *ring, mirror, beside, opposite, above, below]
    for device in partners:
        pl.semaphore_signal(barrier, inc=1, device_id=device, device_id_type=MESH)

    def column(slot):
        wide = jnp.broadcast_to(gain_ref[slot : slot + 1, :], (128, cols)).T
        return jnp.concatenate([wide] * (tokens // 128), axis=1)

    gains = [column(0), column(1)]
    loads["stash1"].wait()
    zg[1] = (stash_ref[1].astype(F32) * gains[1]).astype(BF16)
    loads["cot1"].wait()

    mirror_dy = send(cot_ref.at[1], md, m_s.at[0], m_r.at[0], mirror)
    mirror_z_first = send(zg.at[1], zx, m_s.at[4], m_r.at[4], beside)
    mirror_z = send(zx, mz, m_s.at[1], m_r.at[1], opposite)

    def squares(wide):
        ones = jnp.ones((cols, 128), BF16)
        return dot((wide * wide).astype(BF16), ones, 0, 0)

    core_copies = []
    sums_wide = (two + 128, two, two)

    def core_send(g):
        away = pl.multiple_of((1 - core) * half, half)
        copy = send(
            part.at[g, pl.ds(away, half), : sums_wide[g]],
            r1.at[g, :, : sums_wide[g]],
            core_s.at[g],
            core_r.at[g],
            sibling,
        )
        copy.start()
        core_copies.append(copy)

    def partial_sums(g):
        if g == 0:
            loads["wd"].wait()
            part[0, :, :lat] = dot(zg[1], wd_ref[1], 0, 0).astype(BF16)
            loads["wu"].wait()
            part[0, :, lat:two] = dot(cot_ref[1], wu_ref[1], 0, 0).astype(BF16)
            loads["stash0"].wait()
            loads["fwd"].wait()
            lane = lax.broadcasted_iota(jnp.int32, (tokens, 128), 1)
            norms = squares(stash_ref[1].astype(F32))
            for index, array in enumerate((fwd_ref.at[0], fwd_ref.at[1], stash_ref.at[0])):
                norms = jnp.where(lane < 32 * (index + 1), norms, squares(array[...].astype(F32)))
            part[0, :, two:] = norms.astype(BF16)
        elif g == 2:
            zg[0] = (stash_ref[0].astype(F32) * gains[0]).astype(BF16)
            part[2, :, :lat] = dot(zg[0], wd_ref[0], 0, 0).astype(BF16)
            loads["cot0"].wait()
            part[2, :, lat:two] = dot(cot_ref[0], wu_ref[0], 0, 0).astype(BF16)
        else:
            for slot in range(2):
                rows = (fwd_ref[slot].astype(F32) * gains[slot]).astype(BF16)
                part[1, :, slot * lat : (slot + 1) * lat] = dot(rows, wd_ref[slot], 0, 0).astype(BF16)

    partial_sums(0)
    pl.semaphore_wait(barrier, len(partners))
    mirror_dy.start()
    mirror_z_first.start()
    core_send(0)
    for g in (1, 2):
        partial_sums(g)
        core_send(g)

    def rows_of(index):
        return pl.ds(pl.multiple_of(index * quarter, quarter), quarter)

    y_copies = {}

    def core_sum(g):
        wide = sums_wide[g]
        core_copies[g].wait_recv()
        mine = part[g, pl.ds(pl.multiple_of(core * half, half), half), :wide].astype(F32)
        r1[g, :, :wide] = (mine + r1[g, :, :wide].astype(F32)).astype(BF16)
        for k in range(Y - 1):
            y_copies[g, k] = send(
                r1.at[g, rows_of((y + k + 1) % Y), :wide],
                r2.at[g, k, :, :wide],
                y_s.at[g, k],
                y_r.at[g, k],
                ring[k],
            )
            y_copies[g, k].start()

    x_copies = []

    def y_sum(g):
        wide = sums_wide[g]
        total = r1[g, rows_of(y), :wide].astype(F32)
        for k in range(Y - 1):
            y_copies[g, k].wait_recv()
            total = total + r2[g, k, :, :wide].astype(F32)
        h2[g, :, :wide] = total.astype(BF16)
        copy = send(
            h2.at[g, pl.ds(pl.multiple_of((1 - xh) * own, own), own), :wide],
            r3.at[g, :, :wide],
            x_s.at[g],
            x_r.at[g],
            across,
        )
        copy.start()
        x_copies.append(copy)

    base = pl.multiple_of(core * half + y * quarter + xh * own, own)

    def mean_sq(values):
        return jnp.sum(values * values, axis=1, keepdims=True) / lat

    mirror_rows = send(
        full.at[0, pl.ds(base, own), :two],
        full.at[3, pl.ds(base, own), :two],
        m_s.at[2],
        m_r.at[2],
        mirror,
    )
    gx_copies = {}
    spans = ((lat, two + 128), (0, two), (lat, two + 128), (0, two + lat))

    def gx_send(g):
        spot = full.at[g, pl.ds(base, own), spans[g][0] : spans[g][1]]
        gx_copies[g] = send(spot, spot, gx_s.at[g], gx_r.at[g], across)
        gx_copies[g].start()

    squared = []

    def own_rows(g):
        wide = sums_wide[g]
        x_copies[g].wait_recv()
        total = h2[g, pl.ds(pl.multiple_of(xh * own, own), own), :wide].astype(F32)
        total = total + r3[g, :, :wide].astype(F32)
        first, second = total[:, :lat], total[:, lat:two]
        if g == 0:
            for k in range(4):
                squared.append(total[:, two + 32 * k : two + 32 * k + 1] / features + EPS)
        square = squared[(0, 1, 3)[g]]
        scale = lax.rsqrt(mean_sq(first) + EPS * square)
        unit = first * scale
        if g == 2:
            full[3, pl.ds(base, own), two : two + lat] = unit.astype(BF16)
        else:
            full[g, pl.ds(base, own), :lat] = unit.astype(BF16)
        if g == 1:
            scale = lax.rsqrt(mean_sq(second) + EPS * squared[2])
            full[g, pl.ds(base, own), lat:two] = (second * scale).astype(BF16)
        else:
            mean = jnp.sum(second * unit, axis=1, keepdims=True) / lat
            cot = (scale * (second - unit * mean)).astype(BF16)
            full[g, pl.ds(base, own), lat:two] = cot
            pull = jnp.sum(cot.astype(F32) * first, axis=1, keepdims=True) / (features * square)
            full[g, pl.ds(base, own), two : two + 128] = jnp.broadcast_to(pull, (own, 128)).astype(BF16)
        if g == 0:
            mirror_rows.start()
        gx_send(g)

    gy_copies, gc_copies = {}, {}

    def block_of(index):
        return pl.ds(pl.multiple_of(core * half + index * quarter, quarter), quarter)

    def gc_send(g, index, block):
        spot = full.at[g, block_of(block), spans[g][0] : spans[g][1]]
        gc_copies[g, index] = send(spot, spot, gc_s.at[g, index], gc_r.at[g, index], sibling)
        gc_copies[g, index].start()

    def gy_send(g):
        gx_copies[g].wait_recv()
        spot = full.at[g, block_of(y), spans[g][0] : spans[g][1]]
        for k in range(Y - 1):
            gy_copies[g, k] = send(spot, spot, gy_s.at[g, k], gy_r.at[g, k], ring[k])
            gy_copies[g, k].start()
        gc_send(g, 0, y)

    def gy_pass(g):
        for k in range(1, Y):
            gy_copies[g, k - 1].wait_recv()
            gc_send(g, k, (y + Y - k) % Y)

    def gc_wait(g):
        for k in range(Y):
            gc_copies[g, k].wait_recv()

    ups = (pos < n_pipe - 1, pos > 0)

    def relay(index, slot, out, up):
        return send(rows_out.at[index], out.at[slot], n_s.at[index], n_r.at[index], above if up else below)

    relays = [
        relay(0, 1, bwd_out, True),
        relay(1, 0, bwd_out, False),
        relay(2, 0, fwd_out, True),
        relay(3, 1, fwd_out, False),
    ]

    def relay_start(index):
        @pl.when(ups[index % 2])
        def _():
            relays[index].start()

    mirror_gain = send(gsend, grecv, m_s.at[3], m_r.at[3], mirror)
    pick = jnp.where(lax.broadcasted_iota(jnp.int32, (8, 128), 1) == 0, 1.0, 0.0).astype(BF16)
    gain_parts = {}

    def results(g):
        gc_wait(g)
        if g == 1:
            for slot in range(2):
                branch = dot(wu_ref[slot], full[1, :, slot * lat : (slot + 1) * lat], 1, 1).astype(BF16)
                rows_out[2 + slot] = (fwd_ref[slot].astype(F32) + branch.astype(F32)).astype(BF16)
                relay_start(2 + slot)
            return
        slot = 1 - g // 2
        scaled_cot = dot(wd_ref[slot], full[g, :, lat:two], 1, 1)
        wide = stash_ref[slot].astype(F32)
        pull = dot(pick, full[g, :, two : two + 128], 1, 1)[0:1, :]
        rows_out[1 - slot] = (
            cot_ref[slot].astype(F32) + scaled_cot * gains[slot] - wide * pull
        ).astype(BF16)
        relay_start(1 - slot)
        products = (wide * scaled_cot).astype(BF16)
        gain_parts[slot] = dot(jnp.ones((8, tokens), BF16), products, 1, 1)

    core_sum(0)
    core_sum(1)
    y_sum(0)
    core_sum(2)
    y_sum(1)
    own_rows(0)
    y_sum(2)
    for stage in (own_rows, gy_send, gy_pass):
        for g in range(3):
            if g or stage is not own_rows:
                stage(g)
    mirror_rows.wait_recv()
    mirror_z_first.wait_recv()
    mirror_z.start()
    gx_send(3)
    results(0)
    gy_send(3)
    results(1)
    gy_pass(3)
    results(2)
    gsend[...] = gain_parts[1]
    mirror_gain.start()
    down_acc[...] = dot(zg[0], full[2, :, lat:two], 1, 0)
    gc_wait(3)

    factor = tokens ** (-0.5)
    mirror_dy.wait_recv()
    up = dot(cot_ref[0], full[3, :, two : two + lat], 1, 0) + dot(md[...], full[3, :, :lat], 1, 0)
    gu_out[...] = (up * factor).astype(BF16)
    mirror_z.wait_recv()
    down = down_acc[...] + dot(mz[...], full[3, :, lat:two], 1, 0)
    gd_out[...] = (down * factor).astype(BF16)
    mirror_gain.wait_recv()
    gg_out[...] = ((gain_parts[0] + grecv[...])[0:1, :] * factor).astype(BF16)

    def edge(here, first, second):
        @pl.when(here)
        def _():
            zg[0] = jnp.zeros((cols, tokens), BF16)
            one = pltpu.make_async_copy(zg.at[0], first, zero_sem.at[0])
            other = pltpu.make_async_copy(zg.at[0], second, zero_sem.at[1])
            one.start()
            other.start()
            one.wait()
            other.wait()

    edge(pos == 0, fwd_out.at[0], bwd_out.at[1])
    edge(pos == n_pipe - 1, fwd_out.at[1], bwd_out.at[0])

    for index in range(4):

        @pl.when(ups[index % 2])
        def _():
            relays[index].wait_send()

        @pl.when(ups[1 - index % 2])
        def _():
            relays[index].wait_recv()

    for copy in [
        mirror_dy,
        mirror_z,
        mirror_z_first,
        mirror_rows,
        mirror_gain,
        *core_copies,
        *y_copies.values(),
        *x_copies,
        *gx_copies.values(),
        *gy_copies.values(),
        *gc_copies.values(),
    ]:
        copy.wait_send()


def place(*refs):
    count = len(refs) // 2
    sources, targets, sems = refs[:count], refs[count:-1], refs[-1]
    copies = [
        pltpu.make_async_copy(sources[index], targets[index], sems.at[index]) for index in range(count)
    ]
    for copy in copies:
        copy.start()
    for copy in copies:
        copy.wait()


def per_device(n_pipe, fwd_in, stash, cot_in, w_down, w_up, gain):
    tokens, cols = stash.shape[2:]
    lat = w_down.shape[3]
    wide = 2 * lat + 128
    half, quarter, own = tokens // 2, tokens // 8, tokens // 16
    vmem = pl.BlockSpec(memory_space=pltpu.VMEM)
    anywhere = pl.BlockSpec(memory_space=pl.ANY)
    dma = pltpu.SemaphoreType.DMA
    turned = lambda array: jnp.swapaxes(array[0], 1, 2)
    outs = pl.pallas_call(
        functools.partial(kernel, n_pipe),
        out_shape=(
            jax.ShapeDtypeStruct((2, cols, tokens), BF16),
            jax.ShapeDtypeStruct((2, cols, tokens), BF16),
            jax.ShapeDtypeStruct((cols, lat), BF16),
            jax.ShapeDtypeStruct((cols, lat), BF16),
            jax.ShapeDtypeStruct((1, cols), BF16),
        ),
        in_specs=[anywhere] * 5 + [vmem],
        out_specs=(anywhere, anywhere, vmem, vmem, vmem),
        scratch_shapes=[
            pltpu.VMEM((2, cols, tokens), BF16),
            pltpu.VMEM((2, cols, tokens), BF16),
            pltpu.VMEM((2, cols, tokens), BF16),
            pltpu.VMEM((2, cols, lat), BF16),
            pltpu.VMEM((2, cols, lat), BF16),
            pltpu.VMEM((3, tokens, wide), BF16),
            pltpu.VMEM((3, half, wide), BF16),
            pltpu.VMEM((3, Y - 1, quarter, wide), BF16),
            pltpu.VMEM((3, quarter, wide), BF16),
            pltpu.VMEM((3, own, wide), BF16),
            pltpu.VMEM((4, tokens, 3 * lat), BF16),
            pltpu.VMEM((2, cols, tokens), BF16),
            pltpu.VMEM((cols, tokens), BF16),
            pltpu.VMEM((cols, tokens), BF16),
            pltpu.VMEM((cols, tokens), BF16),
            pltpu.VMEM((8, cols), F32),
            pltpu.VMEM((8, cols), F32),
            pltpu.VMEM((4, cols, tokens), BF16),
            pltpu.VMEM((cols, lat), F32),
            dma((7,)),
            dma((3,)),
            dma((3,)),
            dma((3, Y - 1)),
            dma((3, Y - 1)),
            dma((3,)),
            dma((3,)),
            dma((4,)),
            dma((4,)),
            dma((4, Y - 1)),
            dma((4, Y - 1)),
            dma((4, Y)),
            dma((4, Y)),
            dma((5,)),
            dma((5,)),
            dma((4,)),
            dma((4,)),
            dma((2,)),
        ],
        compiler_params=pltpu.CompilerParams(
            collective_id=0, has_side_effects=True, vmem_limit_bytes=52 * 1024 * 1024
        ),
    )(turned(fwd_in), turned(stash), turned(cot_in), w_down[0], turned(w_up), gain[0])
    fwd_next, bwd_next, grad_down, grad_up, grad_gain = pl.pallas_call(
        place,
        out_shape=tuple(jax.ShapeDtypeStruct(array.shape, array.dtype) for array in outs),
        in_specs=[vmem] * 5,
        out_specs=(anywhere,) * 5,
        scratch_shapes=[dma((5,))],
        compiler_params=pltpu.CompilerParams(vmem_limit_bytes=16 * 1024 * 1024),
    )(*outs)
    return (
        jnp.swapaxes(fwd_next, 1, 2)[None],
        jnp.swapaxes(bwd_next, 1, 2)[None],
        grad_down[None],
        grad_up.T[None],
        grad_gain,
    )


def solution(mesh):
    placed = (
        P("pipe", None, None, "dp"),
        P("pipe", None, None, "dp"),
        P("pipe", None, None, "dp"),
        P("pipe", None, "dp", None),
        P("pipe", None, None, "dp"),
        P("pipe", None, "dp"),
    )
    return jax.shard_map(
        functools.partial(per_device, mesh.shape["pipe"]),
        mesh=mesh,
        in_specs=placed,
        out_specs=(
            P("pipe", None, None, "dp"),
            P("pipe", None, None, "dp"),
            P("pipe", "dp", None),
            P("pipe", None, "dp"),
            P("pipe", "dp"),
        ),
        check_vma=False,
    )
```
